512 devices in a mesh: ctx: 128 (over y_hi, z, x), tp: 4 (over y_lo, core).
Axes of the slice: x: 4, y: 4 (y_hi: 2, y_lo: 2; y = y_hi * 2 + y_lo), z: 16, core: 2. Of those that a mesh axis runs over, the one named last changes fastest.
Arguments:
- gate_query: bfloat16 [16384, 1024], P('ctx', 'tp'), may hold values from -24 to 24, as said below
- key_proj: bfloat16 [16384, 1024], P('ctx', 'tp'), may hold values from -6 to 6
- value_proj: bfloat16 [16384, 1024], P('ctx', 'tp'), may hold values from -6 to 6
- long_filter: float32 [16384, 1024], P('ctx', 'tp'), may hold values from -6 to 6
- out_gain: float32 [1024], P('tp'), may hold values from 0.1 to 1.9
- cotangent: bfloat16 [16384, 1024], P('ctx', 'tp'), may hold values from -24 to 24, as said below
Outputs:
- output: bfloat16 [16384, 1024], P('ctx', 'tp')
- grad_query: bfloat16 [16384, 1024], P('ctx', 'tp')
- grad_key: bfloat16 [16384, 1024], P('ctx', 'tp')
- grad_value: bfloat16 [16384, 1024], P('ctx', 'tp')
- grad_filter: float32 [16384, 1024], P('ctx', 'tp')
- grad_gain: float32 [1024], P('tp')
The draws below stay inside these ranges and needn't reach their ends.
Inputs may be any that keep to these rules, and one draw needn't show every extreme that they name: `gate_query`: real values. `cotangent`: real values.
All inputs are finite; a program needn't handle non-finite values.
Results may differ from the reference program's by a relative error of at most 0.0019.
Values sent between devices are 32-bit elements; how exact they have to be, the bound alone decides.
No kernel may reach another device: no remote copies, remote signals or barrier semaphores. Data moves between devices by JAX's collectives and lax.ppermute only.
A program may use at most 64 MiB of HBM per device.

```python
import math
import jax
import jax.numpy as jnp
from jax import lax

LENGTH = 16384
CHANNELS = 1024


def draw_gate_query(key, part):
    key = jax.random.fold_in(key, 11)
    first_key, second_key = jax.random.split(key)
    column = jnp.arange(CHANNELS, dtype=jnp.float32) / (CHANNELS - 1)
    rough = jax.random.uniform(second_key, (CHANNELS,), jnp.float32, 0.5, 1.5)
    values = jax.random.truncated_normal(first_key, -4.0, 4.0, (LENGTH, CHANNELS), jnp.float32)
    ramp = jnp.exp(jnp.log(3.0) * column)
    return (values * (ramp * rough)[None, :]).astype(jnp.bfloat16)


def draw_cotangent(key, part):
    key = jax.random.fold_in(key, 23)
    first_key, second_key = jax.random.split(key)
    position = jnp.arange(LENGTH, dtype=jnp.float32) / (LENGTH - 1)
    rough = jax.random.uniform(second_key, (LENGTH,), jnp.float32, 0.5, 1.5)
    values = jax.random.truncated_normal(first_key, -4.0, 4.0, (LENGTH, CHANNELS), jnp.float32)
    ramp = jnp.exp(jnp.log(3.0) * position)
    return (values * (ramp * rough)[:, None]).astype(jnp.bfloat16)


def shard_levels(key, extent, cuts, least, largest):
    loudness = 1.0
    for dim, shards_of in cuts:
        heights = jax.random.uniform(jax.random.fold_in(jax.random.fold_in(key, 6), dim), (shards_of,), jnp.float32, least / len(cuts), largest / len(cuts))
        loudness = loudness * jnp.repeat(jnp.exp(heights), extent[dim] // shards_of).reshape((-1,) + (1,) * (len(extent) - 1 - dim))
    return loudness


def noise(stream_key, dims, scale, most, cuts=(), kind=jnp.bfloat16):
    result = scale * jax.random.normal(stream_key, dims, jnp.float32)
    if cuts:
        result = result * shard_levels(stream_key, dims, cuts, -0.22, 0.18)
    return jnp.clip(result, -most, most).astype(kind)


def setup_inputs(seed: int = 0) -> dict:
    key_of = jax.random.split(jax.random.key(seed), 7)
    gate_query = draw_gate_query(jax.random.fold_in(key_of[6], 71), 0)
    key_proj = noise(key_of[1], (LENGTH, CHANNELS), 1.0, 6.0, ((0, 128), (1, 4)))
    value_proj = noise(key_of[2], (LENGTH, CHANNELS), 1.0, 6.0, ((0, 128), (1, 4)))
    long_filter = noise(key_of[3], (LENGTH, CHANNELS), 1.0, 6.0, ((0, 128), (1, 4)), jnp.float32)
    out_gain = jnp.clip(1.0 + 0.18 * jax.random.normal(key_of[4], (CHANNELS,), jnp.float32), 0.1, 1.9)
    cotangent = draw_cotangent(jax.random.fold_in(key_of[6], 71), 0)
    return {"gate_query": gate_query, "key_proj": key_proj, "value_proj": value_proj, "long_filter": long_filter, "out_gain": out_gain, "cotangent": cotangent}


def causal(left_in, right_in):
    length = left_in.shape[0]
    padded = 2 * length
    left_spec = jnp.fft.rfft(left_in, n=padded, axis=0)
    right_spec = jnp.fft.rfft(right_in, n=padded, axis=0)
    return jnp.fft.irfft(left_spec * right_spec, n=padded, axis=0)[:length]

def correlate(left_in, right_in):
    length = left_in.shape[0]
    padded = 2 * length
    left_spec = jnp.fft.rfft(left_in, n=padded, axis=0)
    right_spec = jnp.fft.rfft(right_in, n=padded, axis=0)
    return jnp.fft.irfft(jnp.conj(left_spec) * right_spec, n=padded, axis=0)[:length]

def reference(gate_query, key_proj, value_proj, long_filter, out_gain, cotangent):
    length = gate_query.shape[0]
    filt_scale = 1.0 / math.sqrt(length)
    query_f = gate_query.astype(jnp.float32)
    key_f = key_proj.astype(jnp.float32)
    value_f = value_proj.astype(jnp.float32)
    cot_f = cotangent.astype(jnp.float32)
    mixed_in = key_f * value_f
    filt_in = long_filter * filt_scale
    conv_out = causal(filt_in, mixed_in)
    gated_out = query_f * conv_out
    inv_rms = lax.rsqrt(lax.optimization_barrier(jnp.mean(gated_out * gated_out, axis=1, keepdims=True)) + 1e-06)
    output = (gated_out * inv_rms * out_gain).astype(jnp.bfloat16)
    scaled = cot_f * out_gain
    row_dot = lax.optimization_barrier(jnp.mean(scaled * gated_out, axis=1, keepdims=True))
    grad_gain = lax.optimization_barrier(jnp.sum(cot_f * gated_out * inv_rms, axis=0))
    d_gated = inv_rms * scaled - gated_out * inv_rms * inv_rms * inv_rms * row_dot
    grad_query = (d_gated * conv_out).astype(jnp.bfloat16)
    d_conv = d_gated * query_f
    d_mixed = correlate(filt_in, d_conv)
    grad_key = (d_mixed * value_f).astype(jnp.bfloat16)
    grad_value = (d_mixed * key_f).astype(jnp.bfloat16)
    grad_filter = correlate(mixed_in, d_conv) * filt_scale
    return (output, grad_query, grad_key, grad_value, grad_filter, grad_gain)
```

```python
import functools
import math

import jax
import jax.numpy as jnp
import ml_dtypes
import numpy as np
from jax import lax
from jax.experimental import pallas as pl
from jax.experimental.pallas import tpu as pltpu
from jax.sharding import Mesh, PartitionSpec as P

norm_eps = 1e-06
side = 128
length = side * side
channels = 1024
ctx_axes = ("yh", "z", "x")
ctx_sizes = (2, 16, 4)
tp_axes = ("yl", "core")
tp_sizes = (2, 2)
swap_axes = ("z", "yh", "x")
vmem_bytes = 40 * 1024 * 1024


def split_table(table):
    high = table.astype(np.float32).astype(ml_dtypes.bfloat16)
    low = (table - high.astype(np.float64)).astype(ml_dtypes.bfloat16)
    return np.stack([high, low])


def make_tables():
    order = [ctx_axes.index(name) for name in swap_axes]
    block = np.arange(side).reshape(ctx_sizes).transpose(order).reshape(-1)
    idx = np.arange(side)
    ang_a = 2.0 * math.pi * ((idx[:, None] + 0.25) * block[None, :] / side)
    cos_a, sin_a = np.cos(ang_a), np.sin(ang_a)
    first = np.concatenate([cos_a, sin_a], axis=0)
    scale = 1.0 / length / math.sqrt(length)
    last = np.concatenate([cos_a.T, sin_a.T], axis=1) * scale
    ang_t = 2.0 * math.pi * ((idx[:, None] + 0.25) * idx[None, :] / length)
    twist = np.stack([np.cos(ang_t), np.sin(ang_t)]).astype(np.float32)
    ang_b = 2.0 * math.pi * (idx[:, None] * idx[None, :] % side) / side
    cos_b, sin_b = np.cos(ang_b), np.sin(ang_b)
    ahead = np.block([[cos_b, sin_b], [-sin_b, cos_b]])
    back = np.block([[cos_b, -sin_b], [sin_b, cos_b]])
    return tuple(split_table(t) for t in (first, ahead, back, last)) + (twist,)


def halves(value):
    high = value.astype(jnp.bfloat16)
    low = (value - high.astype(jnp.float32)).astype(jnp.bfloat16)
    return high, low


def dot(left, right):
    return jnp.dot(left, right, preferred_element_type=jnp.float32)


def table_dot(table_ref, value):
    high, low = halves(value)
    return dot(table_ref[0], high) + (dot(table_ref[0], low) + dot(table_ref[1], high))


def dot_table(value, table_ref):
    high, low = halves(value)
    return dot(high, table_ref[0]) + (dot(low, table_ref[0]) + dot(high, table_ref[1]))


def forward_spectra(columns, first_ref, ahead_ref, twist_ref):
    count = len(columns)
    mid = table_dot(first_ref, jnp.concatenate(columns, axis=1))
    cos_t, sin_t = twist_ref[0], twist_ref[1]
    rows = []
    for u in range(count):
        real = mid[:side, u * side : (u + 1) * side]
        imag = mid[side:, u * side : (u + 1) * side]
        rows.append(
            jnp.concatenate([real * cos_t - imag * sin_t, real * sin_t + imag * cos_t], axis=1)
        )
    out = dot_table(jnp.concatenate(rows, axis=0), ahead_ref)
    return [
        (out[u * side : (u + 1) * side, :side], out[u * side : (u + 1) * side, side:])
        for u in range(count)
    ]


def inverse_columns(spectra, back_ref, last_ref, twist_ref):
    count = len(spectra)
    mid = dot_table(
        jnp.concatenate([jnp.concatenate(pair, axis=1) for pair in spectra], axis=0), back_ref
    )
    cos_t, sin_t = twist_ref[0], twist_ref[1]
    cols = []
    for u in range(count):
        real = mid[u * side : (u + 1) * side, :side]
        imag = mid[u * side : (u + 1) * side, side:]
        cols.append(
            jnp.concatenate([real * cos_t + imag * sin_t, imag * cos_t - real * sin_t], axis=0)
        )
    return table_dot(last_ref, jnp.concatenate(cols, axis=1))


def product(left, right):
    return (left[0] * right[0] - left[1] * right[1], left[0] * right[1] + left[1] * right[0])


def conj_product(left, right):
    return (left[0] * right[0] + left[1] * right[1], left[0] * right[1] - left[1] * right[0])


def every(start, stride):
    return pl.ds(start, side, stride=stride)


def send_inputs_kernel(key_ref, value_ref, filt_ref, out_ref):
    mixed = key_ref[...].astype(jnp.float32) * value_ref[...].astype(jnp.float32)
    filt = filt_ref[...]
    for h in range(2):
        cols = slice(h * side, (h + 1) * side)
        out_ref[every(h, 4), :] = filt[:, cols].T
        out_ref[every(2 + h, 4), :] = mixed[:, cols].T


def flip_gates_kernel(query_ref, cot_ref, query_t_ref, cot_t_ref):
    query = query_ref[...].astype(jnp.float32)
    cot = cot_ref[...].astype(jnp.float32)
    for h in range(2):
        cols = slice(h * side, (h + 1) * side)
        query_t_ref[cols, :] = query[:, cols].T
        cot_t_ref[cols, :] = cot[:, cols].T


def conv_kernel(got_ref, first_ref, ahead_ref, back_ref, last_ref, twist_ref, out_ref, spec_ref):
    columns = [got_ref[every(u, 4), :] for u in range(4)]
    spectra = forward_spectra(columns, first_ref, ahead_ref, twist_ref)
    for u in range(4):
        spec_ref[u, 0] = spectra[u][0]
        spec_ref[u, 1] = spectra[u][1]
    both = [product(spectra[h], spectra[2 + h]) for h in range(2)]
    conv = inverse_columns(both, back_ref, last_ref, twist_ref)
    for h in range(2):
        out_ref[every(h, 2), :] = conv[:, h * side : (h + 1) * side]


def row_sums_kernel(conv_ref, query_t_ref, cot_t_ref, gain_ref, out_ref):
    squares = jnp.zeros((1, side), jnp.float32)
    dots = jnp.zeros((1, side), jnp.float32)
    for h in range(2):
        cols = slice(h * side, (h + 1) * side)
        gated = conv_ref[every(h, 2), :] * query_t_ref[cols, :]
        squares = squares + jnp.sum(gated * gated, axis=0, keepdims=True)
        scaled = cot_t_ref[cols, :] * gain_ref[cols, :]
        dots = dots + jnp.sum(scaled * gated, axis=0, keepdims=True)
    out_ref[0:1, :] = squares
    out_ref[1:2, :] = dots


def row_scalars(sums_ref):
    squares = sums_ref[0, 0:1, :]
    dots = sums_ref[0, 1:2, :]
    for t in range(1, 4):
        squares = squares + sums_ref[t, 0:1, :]
        dots = dots + sums_ref[t, 1:2, :]
    inv_rms = lax.rsqrt(squares * (1.0 / channels) + norm_eps)
    return inv_rms, dots * (1.0 / channels)


def d_conv_kernel(conv_ref, query_t_ref, cot_t_ref, gain_ref, sums_ref, out_ref):
    inv_rms, row_dot = row_scalars(sums_ref)
    pull = inv_rms * inv_rms * inv_rms * row_dot
    gains = []
    for h in range(2):
        cols = slice(h * side, (h + 1) * side)
        query = query_t_ref[cols, :]
        cot = cot_t_ref[cols, :]
        gated = conv_ref[every(h, 2), :] * query
        scaled = cot * gain_ref[cols, :]
        out_ref[every(h, 3), :] = (inv_rms * scaled - gated * pull) * query
        gains.append(jnp.sum(cot * gated * inv_rms, axis=1, keepdims=True))
    lane = lax.broadcasted_iota(jnp.int32, (side, side), 1)
    out_ref[every(2, 3), :] = jnp.where(lane < side // 2, gains[0], gains[1])


def row_outputs_kernel(
    conv_ref, query_t_ref, cot_t_ref, gain_ref, sums_ref, gain_row_ref, output_ref, grad_query_ref
):
    inv_rms, row_dot = row_scalars(sums_ref)
    pull = inv_rms * inv_rms * inv_rms * row_dot
    for h in range(2):
        cols = slice(h * side, (h + 1) * side)
        conv = conv_ref[every(h, 2), :]
        gated = conv * query_t_ref[cols, :]
        scaled = cot_t_ref[cols, :] * gain_ref[cols, :]
        normed = (gated * inv_rms).T
        output_ref[:, cols] = (normed * gain_row_ref[:, cols]).astype(jnp.bfloat16)
        grad = (inv_rms * scaled - gated * pull) * conv
        grad_query_ref[:, cols] = grad.T.astype(jnp.bfloat16)


def corr_kernel(
    got_ref, spec_ref, first_ref, ahead_ref, back_ref, last_ref, twist_ref, out_ref
):
    columns = [got_ref[every(h, 3), :] for h in range(2)]
    spectra = forward_spectra(columns, first_ref, ahead_ref, twist_ref)
    pairs = [
        conj_product((spec_ref[u, 0], spec_ref[u, 1]), spectra[u % 2]) for u in range(4)
    ]
    result = inverse_columns(pairs, back_ref, last_ref, twist_ref)
    for u in range(4):
        out_ref[every(u, 5), :] = result[:, u * side : (u + 1) * side]
    gain_sum = jnp.sum(got_ref[every(2, 3), :], axis=0, keepdims=True)
    out_ref[every(4, 5), :] = jnp.broadcast_to(gain_sum, (side, side))


def last_outputs_kernel(
    got_ref, key_ref, value_ref, grad_key_ref, grad_value_ref, grad_filter_ref, grad_gain_ref
):
    gains = got_ref[every(4, 5), :].T
    for h in range(2):
        cols = slice(h * side, (h + 1) * side)
        d_mixed = got_ref[every(h, 5), :].T
        value = value_ref[:, cols].astype(jnp.float32)
        key = key_ref[:, cols].astype(jnp.float32)
        grad_key_ref[:, cols] = (d_mixed * value).astype(jnp.bfloat16)
        grad_value_ref[:, cols] = (d_mixed * key).astype(jnp.bfloat16)
        grad_filter_ref[:, cols] = got_ref[every(2 + h, 5), :].T
        grad_gain_ref[:, cols] = gains[h * (side // 2) : h * (side // 2) + 1, :]


def call(kernel, outs, *operands, flops=0):
    moved = sum(math.prod(o.shape) * o.dtype.itemsize for o in operands)
    moved += sum(math.prod(o.shape) * o.dtype.itemsize for o in outs)
    result = pl.pallas_call(
        kernel,
        out_shape=outs,
        compiler_params=pltpu.CompilerParams(vmem_limit_bytes=vmem_bytes),
        cost_estimate=pl.CostEstimate(flops=flops, bytes_accessed=moved, transcendentals=0),
    )(*operands)
    return result


def f32(*shape):
    return jax.ShapeDtypeStruct(shape, jnp.float32)


def bf16(*shape):
    return jax.ShapeDtypeStruct(shape, jnp.bfloat16)


def swap(sent, rows):
    got = lax.all_to_all(
        sent.reshape(side, 1, rows * side), swap_axes, split_axis=0, concat_axis=0, tiled=True
    )
    return got.reshape(side * rows, side)


def per_device(gate_query, key_proj, value_proj, long_filter, out_gain, cotangent):
    first, ahead, back, last, twist = (jnp.asarray(t) for t in make_tables())
    wide = 2 * side
    gain_row = out_gain.reshape(1, wide)
    gain_col = jnp.broadcast_to(out_gain[:, None], (wide, side))

    (sent,) = call(send_inputs_kernel, (f32(4 * side, side),), key_proj, value_proj, long_filter)
    got = swap(sent, 4)
    query_t, cot_t = call(
        flip_gates_kernel, (f32(wide, side), f32(wide, side)), gate_query, cotangent
    )
    sent, spectra = call(
        conv_kernel,
        (f32(wide, side), f32(4, 2, side, side)),
        got,
        first,
        ahead,
        back,
        last,
        twist,
    )
    conv_t = swap(sent, 2)
    (sums,) = call(row_sums_kernel, (f32(2, side),), conv_t, query_t, cot_t, gain_col)
    sums = lax.all_gather(sums, tp_axes)
    (sent,) = call(d_conv_kernel, (f32(3 * side, side),), conv_t, query_t, cot_t, gain_col, sums)
    got = swap(sent, 3)
    output, grad_query = call(
        row_outputs_kernel,
        (bf16(side, wide), bf16(side, wide)),
        conv_t,
        query_t,
        cot_t,
        gain_col,
        sums,
        gain_row,
    )
    (sent,) = call(
        corr_kernel,
        (f32(5 * side, side),),
        got,
        spectra,
        first,
        ahead,
        back,
        last,
        twist,
    )
    got = swap(sent, 5)
    grad_key, grad_value, grad_filter, grad_gain = call(
        last_outputs_kernel,
        (bf16(side, wide), bf16(side, wide), f32(side, wide), f32(1, wide)),
        got,
        key_proj,
        value_proj,
    )
    return (output, grad_query, grad_key, grad_value, grad_filter, grad_gain.reshape(wide))


def solution(mesh):
    fine = Mesh(mesh.devices.reshape(ctx_sizes + tp_sizes), ctx_axes + tp_axes)
    both = P(ctx_axes, tp_axes)
    return jax.shard_map(
        per_device,
        mesh=fine,
        in_specs=(both, both, both, both, P(tp_axes), both),
        out_specs=(both, both, both, both, both, P(tp_axes)),
        check_vma=False,
    )
```

```python
import math

import jax
import jax.numpy as jnp
import numpy as np
from jax import lax
from jax.experimental import pallas as pl
from jax.experimental.pallas import tpu as pltpu
from jax.sharding import PartitionSpec as P

norm_eps = 1e-06
side = 128
length = side * side
channels = 1024
ctx_sizes = (2, 16, 4)
vmem_bytes = 40 * 1024 * 1024


def swap_order():
    grid = np.arange(side).reshape(ctx_sizes).transpose(1, 2, 0)
    return np.roll(grid, (8, 2, 1), axis=(0, 1, 2)).reshape(-1).tolist()


def make_tables():
    block = np.array(swap_order())
    idx = np.arange(side)
    ang_a = 2.0 * math.pi * ((idx[:, None] + 0.25) * block[None, :] / side)
    cos_a, sin_a = np.cos(ang_a), np.sin(ang_a)
    first = np.concatenate([cos_a, sin_a], axis=0)
    scale = 1.0 / length / math.sqrt(length)
    last = np.concatenate([cos_a.T, sin_a.T], axis=1) * scale
    ang_t = 2.0 * math.pi * ((idx[:, None] + 0.25) * idx[None, :] / length)
    twist = np.stack([np.cos(ang_t), np.sin(ang_t)]).astype(np.float32)
    ang_b = 2.0 * math.pi * (idx[:, None] * idx[None, :] % side) / side
    cos_b, sin_b = np.cos(ang_b), np.sin(ang_b)
    ahead = np.block([[cos_b, sin_b], [-sin_b, cos_b]])
    back = np.block([[cos_b, -sin_b], [sin_b, cos_b]])
    return tuple(t.astype(np.float32) for t in (first, ahead, back, last)) + (twist,)


def halves(value):
    high = value.astype(jnp.bfloat16)
    low = (value - high.astype(jnp.float32)).astype(jnp.bfloat16)
    return high, low


def dot(left, right):
    return jnp.dot(left, right, preferred_element_type=jnp.float32)


def split_kernel(*refs):
    count = len(refs) // 3
    for i in range(count):
        high, low = halves(refs[i][...])
        refs[count + 2 * i][...] = high
        refs[count + 2 * i + 1][...] = low


def exact_dot(left, right):
    (left_high, left_low), (right_high, right_low) = left, right
    return dot(left_high, right_high) + (dot(left_high, right_low) + dot(left_low, right_high))


def load(pair):
    return pair[0][...], pair[1][...]


def forward_spectra(columns, first, ahead, twist_ref):
    count = len(columns)
    mid = exact_dot(load(first), halves(jnp.concatenate(columns, axis=1)))
    cos_t, sin_t = twist_ref[0], twist_ref[1]
    rows = []
    for u in range(count):
        real = mid[:side, u * side : (u + 1) * side]
        imag = mid[side:, u * side : (u + 1) * side]
        rows.append(
            jnp.concatenate([real * cos_t - imag * sin_t, real * sin_t + imag * cos_t], axis=1)
        )
    out = exact_dot(halves(jnp.concatenate(rows, axis=0)), load(ahead))
    return [
        (out[u * side : (u + 1) * side, :side], out[u * side : (u + 1) * side, side:])
        for u in range(count)
    ]


def inverse_columns(spectra, back, last, twist_ref):
    count = len(spectra)
    stacked = jnp.concatenate([jnp.concatenate(pair, axis=1) for pair in spectra], axis=0)
    mid = exact_dot(halves(stacked), load(back))
    cos_t, sin_t = twist_ref[0], twist_ref[1]
    cols = []
    for u in range(count):
        real = mid[u * side : (u + 1) * side, :side]
        imag = mid[u * side : (u + 1) * side, side:]
        cols.append(
            jnp.concatenate([real * cos_t + imag * sin_t, imag * cos_t - real * sin_t], axis=0)
        )
    return exact_dot(load(last), halves(jnp.concatenate(cols, axis=1)))


def product(left, right):
    return (left[0] * right[0] - left[1] * right[1], left[0] * right[1] + left[1] * right[0])


def conj_product(left, right):
    return (left[0] * right[0] + left[1] * right[1], left[0] * right[1] - left[1] * right[0])


def every(start, stride):
    return pl.ds(start, side, stride=stride)


def send_inputs_kernel(key_hbm, value_hbm, filt_hbm, out_ref, key_ref, value_ref, filt_ref, sems):
    pairs = ((key_hbm, key_ref), (value_hbm, value_ref), (filt_hbm, filt_ref))
    copies = [pltpu.make_async_copy(a, b, sems.at[i]) for i, (a, b) in enumerate(pairs)]
    for copy in copies:
        copy.start()
    for copy in copies:
        copy.wait()
    mixed = key_ref[...].astype(jnp.float32) * value_ref[...].astype(jnp.float32)
    filt = filt_ref[...]
    for h in range(2):
        cols = slice(h * side, (h + 1) * side)
        out_ref[every(h, 4), :] = filt[:, cols].T
        out_ref[every(2 + h, 4), :] = mixed[:, cols].T


def flip_gates_kernel(query_ref, cot_ref, gain_ref, query_t_ref, cot_t_ref, scaled_t_ref):
    query = query_ref[...].astype(jnp.float32)
    cot = cot_ref[...].astype(jnp.float32)
    scaled = cot * gain_ref[...]
    for h in range(2):
        cols = slice(h * side, (h + 1) * side)
        query_t_ref[cols, :] = query[:, cols].T
        cot_t_ref[cols, :] = cot[:, cols].T
        scaled_t_ref[cols, :] = scaled[:, cols].T


def conv_kernel(got_ref, *refs):
    first, ahead, back, last = (refs[i : i + 2] for i in range(0, 8, 2))
    twist_ref, out_ref, spec_ref = refs[8:]
    columns = [got_ref[every(u, 4), :] for u in range(4)]
    spectra = forward_spectra(columns, first, ahead, twist_ref)
    for u in range(4):
        spec_ref[u, 0] = spectra[u][0]
        spec_ref[u, 1] = spectra[u][1]
    both = [product(spectra[h], spectra[2 + h]) for h in range(2)]
    conv = inverse_columns(both, back, last, twist_ref)
    for h in range(2):
        out_ref[every(h, 2), :] = conv[:, h * side : (h + 1) * side]


def row_sums_kernel(conv_ref, query_t_ref, scaled_t_ref, out_ref):
    squares = jnp.zeros((1, side), jnp.float32)
    dots = jnp.zeros((1, side), jnp.float32)
    for h in range(2):
        cols = slice(h * side, (h + 1) * side)
        gated = conv_ref[every(h, 2), :] * query_t_ref[cols, :]
        squares = squares + jnp.sum(gated * gated, axis=0, keepdims=True)
        dots = dots + jnp.sum(scaled_t_ref[cols, :] * gated, axis=0, keepdims=True)
    out_ref[0:1, :] = squares
    out_ref[1:2, :] = dots


def row_scalars(sums_ref):
    squares = sums_ref[0, 0:1, :]
    dots = sums_ref[0, 1:2, :]
    for t in range(1, 4):
        squares = squares + sums_ref[t, 0:1, :]
        dots = dots + sums_ref[t, 1:2, :]
    inv_rms = lax.rsqrt(squares * (1.0 / channels) + norm_eps)
    return inv_rms, dots * (1.0 / channels)


def d_conv_kernel(conv_ref, query_t_ref, cot_t_ref, scaled_t_ref, sums_ref, out_ref):
    inv_rms, row_dot = row_scalars(sums_ref)
    pull = inv_rms * inv_rms * inv_rms * row_dot
    parts = []
    for h in range(2):
        cols = slice(h * side, (h + 1) * side)
        query = query_t_ref[cols, :]
        cot = cot_t_ref[cols, :]
        gated = conv_ref[every(h, 2), :] * query
        scaled = scaled_t_ref[cols, :]
        out_ref[every(h, 3), :] = (inv_rms * scaled - gated * pull) * query
        part = jnp.sum(cot * gated * inv_rms, axis=1, keepdims=True)
        parts.append(jnp.broadcast_to(part, (side, side)).T)
    number = lax.broadcasted_iota(jnp.int32, (side, side), 0)
    out_ref[every(2, 3), :] = jnp.where((number & 2) == 0, parts[0], parts[1])


def row_outputs_kernel(
    conv_ref,
    query_t_ref,
    scaled_t_ref,
    sums_ref,
    gain_ref,
    got_ref,
    output_ref,
    grad_query_ref,
    gain_half_ref,
):
    inv_rms, row_dot = row_scalars(sums_ref)
    pull = inv_rms * inv_rms * inv_rms * row_dot
    for h in range(2):
        cols = slice(h * side, (h + 1) * side)
        conv = conv_ref[every(h, 2), :]
        gated = conv * query_t_ref[cols, :]
        scaled = scaled_t_ref[cols, :]
        normed = (gated * inv_rms).T
        output_ref[:, cols] = (normed * gain_ref[:, cols]).astype(jnp.bfloat16)
        grad = (inv_rms * scaled - gated * pull) * conv
        grad_query_ref[:, cols] = grad.T.astype(jnp.bfloat16)
    gain_half_ref[...] = jnp.sum(got_ref[every(2, 3), :], axis=0, keepdims=True)


def corr_kernel(got_ref, spec_ref, *refs):
    first, ahead, back, last = (refs[i : i + 2] for i in range(0, 8, 2))
    twist_ref, out_ref = refs[8:]
    columns = [got_ref[every(h, 3), :] for h in range(2)]
    spectra = forward_spectra(columns, first, ahead, twist_ref)
    pairs = [
        conj_product((spec_ref[u, 0], spec_ref[u, 1]), spectra[u % 2]) for u in range(4)
    ]
    result = inverse_columns(pairs, back, last, twist_ref)
    for u in range(4):
        out_ref[every(u, 4), :] = result[:, u * side : (u + 1) * side]


def last_outputs_kernel(
    got_ref, key_ref, value_ref, grad_key_ref, grad_value_ref, grad_filter_ref
):
    for h in range(2):
        cols = slice(h * side, (h + 1) * side)
        d_mixed = got_ref[every(h, 4), :].T
        value = value_ref[:, cols].astype(jnp.float32)
        key = key_ref[:, cols].astype(jnp.float32)
        grad_key_ref[:, cols] = (d_mixed * value).astype(jnp.bfloat16)
        grad_value_ref[:, cols] = (d_mixed * key).astype(jnp.bfloat16)
        grad_filter_ref[:, cols] = got_ref[every(2 + h, 4), :].T


def call(kernel, outs, *operands, limit=vmem_bytes, **options):
    moved = sum(math.prod(o.shape) * o.dtype.itemsize for o in operands)
    moved += sum(math.prod(o.shape) * o.dtype.itemsize for o in outs)
    result = pl.pallas_call(
        kernel,
        out_shape=outs,
        compiler_params=pltpu.CompilerParams(vmem_limit_bytes=limit),
        cost_estimate=pl.CostEstimate(flops=0, bytes_accessed=moved, transcendentals=0),
        **options,
    )(*operands)
    return result


def f32(*shape):
    return jax.ShapeDtypeStruct(shape, jnp.float32)


def bf16(*shape):
    return jax.ShapeDtypeStruct(shape, jnp.bfloat16)


def swap(sent, rows):
    shape = (side, 1, rows * side) if rows == 3 else (side, rows, side)
    got = lax.all_to_all(
        sent.reshape(shape),
        "ctx",
        split_axis=0,
        concat_axis=0,
        axis_index_groups=[swap_order()],
        tiled=True,
    )
    return got.reshape(side * rows, side)


def per_device(gate_query, key_proj, value_proj, long_filter, out_gain, cotangent):
    *tables, twist = (jnp.asarray(t) for t in make_tables())
    wide = 2 * side
    gain = out_gain.reshape(1, wide)

    in_hbm = pl.BlockSpec(memory_space=pltpu.HBM)
    (sent,) = call(
        send_inputs_kernel,
        (f32(4 * side, side),),
        key_proj,
        value_proj,
        long_filter,
        limit=None,
        in_specs=[in_hbm] * 3,
        scratch_shapes=[
            pltpu.VMEM((side, wide), jnp.bfloat16),
            pltpu.VMEM((side, wide), jnp.bfloat16),
            pltpu.VMEM((side, wide), jnp.float32),
            pltpu.SemaphoreType.DMA((3,)),
        ],
    )
    got = swap(sent, 4)
    tables = call(
        split_kernel, tuple(bf16(*t.shape) for t in tables for _ in range(2)), *tables
    )
    query_t, cot_t, scaled_t = call(
        flip_gates_kernel, (f32(wide, side),) * 3, gate_query, cotangent, gain
    )
    sent, spectra = call(
        conv_kernel,
        (f32(wide, side), f32(4, 2, side, side)),
        got,
        *tables,
        twist,
    )
    conv_t = swap(sent, 2)
    (sums,) = call(row_sums_kernel, (f32(2, side),), conv_t, query_t, scaled_t)
    sums = lax.all_gather(sums, "tp")
    (sent,) = call(d_conv_kernel, (f32(3 * side, side),), conv_t, query_t, cot_t, scaled_t, sums)
    got = swap(sent, 3)
    output, grad_query, gain_half = call(
        row_outputs_kernel,
        (bf16(side, wide), bf16(side, wide), f32(1, side)),
        conv_t,
        query_t,
        scaled_t,
        sums,
        gain,
        got,
    )
    other_half = lax.ppermute(gain_half, "ctx", [(i, i ^ 1) for i in range(side)])
    odd = (lax.axis_index("ctx") & 1) == 1
    grad_gain = jnp.concatenate(
        [jnp.where(odd, other_half, gain_half), jnp.where(odd, gain_half, other_half)], axis=1
    )
    (sent,) = call(
        corr_kernel,
        (f32(4 * side, side),),
        got,
        spectra,
        *tables,
        twist,
    )
    got = swap(sent, 4)
    grad_key, grad_value, grad_filter = call(
        last_outputs_kernel,
        (bf16(side, wide), bf16(side, wide), f32(side, wide)),
        got,
        key_proj,
        value_proj,
    )
    return (output, grad_query, grad_key, grad_value, grad_filter, grad_gain.reshape(wide))


def solution(mesh):
    both = P("ctx", "tp")
    return jax.shard_map(
        per_device,
        mesh=mesh,
        in_specs=(both, both, both, both, P("tp"), both),
        out_specs=(both, both, both, both, both, P("tp")),
        check_vma=False,
    )
```

```python
import math

import jax
import jax.numpy as jnp
import numpy as np
from jax import lax
from jax.experimental import pallas as pl
from jax.experimental.pallas import tpu as pltpu
from jax.sharding import PartitionSpec as P

norm_eps = 1e-06
side = 128
length = side * side
channels = 1024
ctx_sizes = (2, 16, 4)
vmem_bytes = 40 * 1024 * 1024


def swap_order():
    grid = np.arange(side).reshape(ctx_sizes).transpose(1, 2, 0)
    return np.roll(grid, (8, 2, 1), axis=(0, 1, 2)).reshape(-1).tolist()


def make_tables():
    block = np.array(swap_order())
    idx = np.arange(side)
    ang_a = 2.0 * math.pi * ((idx[:, None] + 0.25) * block[None, :] / side)
    cos_a, sin_a = np.cos(ang_a), np.sin(ang_a)
    first = np.concatenate([cos_a, sin_a], axis=0)
    scale = 1.0 / length / math.sqrt(length)
    last = np.concatenate([cos_a.T, sin_a.T], axis=1) * scale
    ang_t = 2.0 * math.pi * ((idx[:, None] + 0.25) * idx[None, :] / length)
    twist = np.stack([np.cos(ang_t), np.sin(ang_t)]).astype(np.float32)
    ang_b = 2.0 * math.pi * (idx[:, None] * idx[None, :] % side) / side
    cos_b, sin_b = np.cos(ang_b), np.sin(ang_b)
    ahead = np.block([[cos_b, sin_b], [-sin_b, cos_b]])
    back = np.block([[cos_b, -sin_b], [sin_b, cos_b]])
    return tuple(t.astype(np.float32) for t in (first, ahead, back, last)) + (twist,)


def halves(value):
    high = value.astype(jnp.bfloat16)
    low = (value - high.astype(jnp.float32)).astype(jnp.bfloat16)
    return high, low


def dot(left, right):
    return jnp.dot(left, right, preferred_element_type=jnp.float32)


def exact_dot(left, right):
    (left_high, left_low), (right_high, right_low) = left, right
    return dot(left_high, right_high) + (dot(left_high, right_low) + dot(left_low, right_high))


def forward_spectra(columns, first_ref, ahead_ref, twist_ref):
    count = len(columns)
    high, low = halves(jnp.concatenate(columns, axis=1))
    first_high, first_low = halves(first_ref[...])
    mid = dot(jnp.concatenate([first_high, first_high], axis=1), jnp.concatenate([high, low], axis=0))
    mid = mid + dot(first_low, high)
    cos_t, sin_t = twist_ref[0], twist_ref[1]
    rows = []
    for u in range(count):
        real = mid[:side, u * side : (u + 1) * side]
        imag = mid[side:, u * side : (u + 1) * side]
        rows.append(
            jnp.concatenate([real * cos_t - imag * sin_t, real * sin_t + imag * cos_t], axis=1)
        )
    out = exact_dot(halves(jnp.concatenate(rows, axis=0)), halves(ahead_ref[...]))
    return [
        (out[u * side : (u + 1) * side, :side], out[u * side : (u + 1) * side, side:])
        for u in range(count)
    ]


def inverse_columns(spectra, back_ref, last_ref, twist_ref):
    count = len(spectra)
    stacked = jnp.concatenate([jnp.concatenate(pair, axis=1) for pair in spectra], axis=0)
    mid = exact_dot(halves(stacked), halves(back_ref[...]))
    cos_t, sin_t = twist_ref[0], twist_ref[1]
    cols = []
    for u in range(count):
        real = mid[u * side : (u + 1) * side, :side]
        imag = mid[u * side : (u + 1) * side, side:]
        cols.append(
            jnp.concatenate([real * cos_t + imag * sin_t, imag * cos_t - real * sin_t], axis=0)
        )
    return exact_dot(halves(last_ref[...]), halves(jnp.concatenate(cols, axis=1)))


def product(left, right):
    return (left[0] * right[0] - left[1] * right[1], left[0] * right[1] + left[1] * right[0])


def conj_product(left, right):
    return (left[0] * right[0] + left[1] * right[1], left[0] * right[1] - left[1] * right[0])


def every(start, stride):
    return pl.ds(start, side, stride=stride)


def first_kernel(key_hbm, value_hbm, filt_hbm, query_hbm, cot_hbm, gain_hbm, *refs):
    sent_ref, query_t_ref, cot_t_ref, scaled_t_ref = refs[:4]
    key_ref, value_ref, filt_ref, query_ref, cot_ref, gain_ref, sems = refs[4:]
    sources = (filt_hbm, key_hbm, value_hbm, query_hbm, cot_hbm, gain_hbm)
    targets = (filt_ref, key_ref, value_ref, query_ref, cot_ref, gain_ref)
    copies = [
        pltpu.make_async_copy(a, b, sems.at[i]) for i, (a, b) in enumerate(zip(sources, targets))
    ]
    for copy in copies:
        copy.start()
    halves_of = [slice(h * side, (h + 1) * side) for h in range(2)]
    copies[0].wait()
    for h, cols in enumerate(halves_of):
        sent_ref[every(h, 4), :] = filt_ref[:, cols].T
    copies[1].wait()
    copies[2].wait()
    for h, cols in enumerate(halves_of):
        mixed = key_ref[:, cols].astype(jnp.float32) * value_ref[:, cols].astype(jnp.float32)
        sent_ref[every(2 + h, 4), :] = mixed.T
    for copy in copies[3:]:
        copy.wait()
    for h, cols in enumerate(halves_of):
        cot = cot_ref[:, cols].astype(jnp.float32)
        query_t_ref[cols, :] = query_ref[:, cols].astype(jnp.float32).T
        cot_t_ref[cols, :] = cot.T
        scaled_t_ref[cols, :] = (cot * gain_ref[:, cols]).T


def conv_kernel(got_ref, first_ref, ahead_ref, back_ref, last_ref, twist_ref, out_ref, spec_ref):
    columns = [got_ref[every(u, 4), :] for u in range(4)]
    spectra = forward_spectra(columns, first_ref, ahead_ref, twist_ref)
    for u in range(4):
        spec_ref[u, 0] = spectra[u][0]
        spec_ref[u, 1] = spectra[u][1]
    both = [product(spectra[h], spectra[2 + h]) for h in range(2)]
    conv = inverse_columns(both, back_ref, last_ref, twist_ref)
    for h in range(2):
        out_ref[every(h, 2), :] = conv[:, h * side : (h + 1) * side]


def row_sums_kernel(conv_ref, query_t_ref, scaled_t_ref, out_ref):
    squares = jnp.zeros((1, side), jnp.float32)
    dots = jnp.zeros((1, side), jnp.float32)
    for h in range(2):
        cols = slice(h * side, (h + 1) * side)
        gated = conv_ref[every(h, 2), :] * query_t_ref[cols, :]
        squares = squares + jnp.sum(gated * gated, axis=0, keepdims=True)
        dots = dots + jnp.sum(scaled_t_ref[cols, :] * gated, axis=0, keepdims=True)
    out_ref[0:1, :] = squares
    out_ref[1:2, :] = dots


def row_scalars(sums_ref):
    squares = sums_ref[0, 0:1, :]
    dots = sums_ref[0, 1:2, :]
    for t in range(1, 4):
        squares = squares + sums_ref[t, 0:1, :]
        dots = dots + sums_ref[t, 1:2, :]
    inv_rms = lax.rsqrt(squares * (1.0 / channels) + norm_eps)
    return inv_rms, dots * (1.0 / channels)


def d_conv_kernel(conv_ref, query_t_ref, cot_t_ref, scaled_t_ref, sums_ref, out_ref):
    inv_rms, row_dot = row_scalars(sums_ref)
    pull = inv_rms * inv_rms * inv_rms * row_dot
    parts = []
    for h in range(2):
        cols = slice(h * side, (h + 1) * side)
        query = query_t_ref[cols, :]
        cot = cot_t_ref[cols, :]
        gated = conv_ref[every(h, 2), :] * query
        scaled = scaled_t_ref[cols, :]
        out_ref[every(h, 3), :] = (inv_rms * scaled - gated * pull) * query
        part = jnp.sum(cot * gated * inv_rms, axis=1, keepdims=True)
        parts.append(jnp.broadcast_to(part, (side, side)).T)
    number = lax.broadcasted_iota(jnp.int32, (side, side), 0)
    out_ref[every(2, 3), :] = jnp.where((number & 2) == 0, parts[0], parts[1])


def row_outputs_kernel(
    conv_ref,
    query_t_ref,
    scaled_t_ref,
    sums_ref,
    gain_ref,
    got_ref,
    output_ref,
    grad_query_ref,
    gain_half_ref,
):
    inv_rms, row_dot = row_scalars(sums_ref)
    pull = inv_rms * inv_rms * inv_rms * row_dot
    for h in range(2):
        cols = slice(h * side, (h + 1) * side)
        conv = conv_ref[every(h, 2), :]
        gated = conv * query_t_ref[cols, :]
        scaled = scaled_t_ref[cols, :]
        normed = (gated * inv_rms).T
        output_ref[:, cols] = (normed * gain_ref[:, cols]).astype(jnp.bfloat16)
        grad = (inv_rms * scaled - gated * pull) * conv
        grad_query_ref[:, cols] = grad.T.astype(jnp.bfloat16)
    gain_half_ref[...] = jnp.sum(got_ref[every(2, 3), :], axis=0, keepdims=True)


def corr_kernel(
    got_ref, spec_ref, first_ref, ahead_ref, back_ref, last_ref, twist_ref, out_ref
):
    columns = [got_ref[every(h, 3), :] for h in range(2)]
    spectra = forward_spectra(columns, first_ref, ahead_ref, twist_ref)
    pairs = [
        conj_product((spec_ref[u, 0], spec_ref[u, 1]), spectra[u % 2]) for u in range(4)
    ]
    result = inverse_columns(pairs, back_ref, last_ref, twist_ref)
    for u in range(4):
        out_ref[every(u, 4), :] = result[:, u * side : (u + 1) * side]


def last_outputs_kernel(
    got_ref, key_ref, value_ref, grad_key_ref, grad_value_ref, grad_filter_ref
):
    for h in range(2):
        cols = slice(h * side, (h + 1) * side)
        d_mixed = got_ref[every(h, 4), :].T
        value = value_ref[:, cols].astype(jnp.float32)
        key = key_ref[:, cols].astype(jnp.float32)
        grad_key_ref[:, cols] = (d_mixed * value).astype(jnp.bfloat16)
        grad_value_ref[:, cols] = (d_mixed * key).astype(jnp.bfloat16)
        grad_filter_ref[:, cols] = got_ref[every(2 + h, 4), :].T


def call(kernel, outs, *operands, **options):
    moved = sum(math.prod(o.shape) * o.dtype.itemsize for o in operands)
    moved += sum(math.prod(o.shape) * o.dtype.itemsize for o in outs)
    result = pl.pallas_call(
        kernel,
        out_shape=outs,
        compiler_params=pltpu.CompilerParams(vmem_limit_bytes=vmem_bytes),
        cost_estimate=pl.CostEstimate(flops=0, bytes_accessed=moved, transcendentals=0),
        **options,
    )(*operands)
    return result


def f32(*shape):
    return jax.ShapeDtypeStruct(shape, jnp.float32)


def bf16(*shape):
    return jax.ShapeDtypeStruct(shape, jnp.bfloat16)


def swap(sent, rows):
    shape = (side, 1, rows * side) if rows == 3 else (side, rows, side)
    got = lax.all_to_all(
        sent.reshape(shape),
        "ctx",
        split_axis=0,
        concat_axis=0,
        axis_index_groups=[swap_order()],
        tiled=True,
    )
    return got.reshape(side * rows, side)


def per_device(gate_query, key_proj, value_proj, long_filter, out_gain, cotangent):
    *tables, twist = (jnp.asarray(t) for t in make_tables())
    wide = 2 * side
    gain = out_gain.reshape(1, wide)

    in_hbm = pl.BlockSpec(memory_space=pltpu.HBM)
    inputs = (key_proj, value_proj, long_filter, gate_query, cotangent, gain)
    sent, query_t, cot_t, scaled_t = call(
        first_kernel,
        (f32(4 * side, side),) + (f32(wide, side),) * 3,
        *(pltpu.with_memory_space_constraint(x, pltpu.HBM) for x in inputs),
        in_specs=[in_hbm] * 6,
        scratch_shapes=[
            pltpu.VMEM((side, wide), jnp.bfloat16),
            pltpu.VMEM((side, wide), jnp.bfloat16),
            pltpu.VMEM((side, wide), jnp.float32),
            pltpu.VMEM((side, wide), jnp.bfloat16),
            pltpu.VMEM((side, wide), jnp.bfloat16),
            pltpu.VMEM((1, wide), jnp.float32),
            pltpu.SemaphoreType.DMA((6,)),
        ],
    )
    got = swap(sent, 4)
    sent, spectra = call(
        conv_kernel, (f32(wide, side), f32(4, 2, side, side)), got, *tables, twist
    )
    conv_t = swap(sent, 2)
    (sums,) = call(row_sums_kernel, (f32(2, side),), conv_t, query_t, scaled_t)
    sums = lax.all_gather(sums, "tp")
    (sent,) = call(d_conv_kernel, (f32(3 * side, side),), conv_t, query_t, cot_t, scaled_t, sums)
    got = swap(sent, 3)
    output, grad_query, gain_half = call(
        row_outputs_kernel,
        (bf16(side, wide), bf16(side, wide), f32(1, side)),
        conv_t,
        query_t,
        scaled_t,
        sums,
        gain,
        got,
    )
    other_half = lax.ppermute(gain_half, "ctx", [(i, i ^ 1) for i in range(side)])
    odd = (lax.axis_index("ctx") & 1) == 1
    grad_gain = jnp.concatenate(
        [jnp.where(odd, other_half, gain_half), jnp.where(odd, gain_half, other_half)], axis=1
    )
    (sent,) = call(
        corr_kernel,
        (f32(4 * side, side),),
        got,
        spectra,
        *tables,
        twist,
    )
    got = swap(sent, 4)
    grad_key, grad_value, grad_filter = call(
        last_outputs_kernel,
        (bf16(side, wide), bf16(side, wide), f32(side, wide)),
        got,
        key_proj,
        value_proj,
    )
    return (output, grad_query, grad_key, grad_value, grad_filter, grad_gain.reshape(wide))


def solution(mesh):
    both = P("ctx", "tp")
    return jax.shard_map(
        per_device,
        mesh=mesh,
        in_specs=(both, both, both, both, P("tp"), both),
        out_specs=(both, both, both, both, both, P("tp")),
        check_vma=False,
    )
```

```python
import math

import jax
import jax.numpy as jnp
import numpy as np
from jax import lax
from jax.experimental import pallas as pl
from jax.experimental.pallas import tpu as pltpu
from jax.sharding import PartitionSpec as P

norm_eps = 1e-06
side = 128
length = side * side
channels = 1024
ctx_sizes = (2, 16, 4)
vmem_bytes = 40 * 1024 * 1024


def swap_order():
    grid = np.arange(side).reshape(ctx_sizes).transpose(1, 2, 0)
    return np.roll(grid, (8, 2, 1), axis=(0, 1, 2)).reshape(-1).tolist()


def make_tables():
    block = np.array(swap_order())
    idx = np.arange(side)
    ang_a = 2.0 * math.pi * ((idx[:, None] + 0.25) * block[None, :] / side)
    cos_a, sin_a = np.cos(ang_a), np.sin(ang_a)
    first = np.concatenate([cos_a, sin_a], axis=0)
    scale = 1.0 / length / math.sqrt(length)
    last = np.concatenate([cos_a.T, sin_a.T], axis=1) * scale
    ang_t = 2.0 * math.pi * ((idx[:, None] + 0.25) * idx[None, :] / length)
    twist = np.stack([np.cos(ang_t), np.sin(ang_t)]).astype(np.float32)
    ang_b = 2.0 * math.pi * (idx[:, None] * idx[None, :] % side) / side
    cos_b, sin_b = np.cos(ang_b), np.sin(ang_b)
    ahead = np.block([[cos_b, sin_b], [-sin_b, cos_b]])
    back = np.block([[cos_b, -sin_b], [sin_b, cos_b]])
    return tuple(t.astype(np.float32) for t in (first, ahead, back, last)) + (twist,)


def halves(value):
    high = value.astype(jnp.bfloat16)
    low = (value - high.astype(jnp.float32)).astype(jnp.bfloat16)
    return high, low


def dot(left, right):
    return jnp.dot(left, right, preferred_element_type=jnp.float32)


def exact_dot(left, right):
    (left_high, left_low), (right_high, right_low) = left, right
    return dot(left_high, right_high) + (dot(left_high, right_low) + dot(left_low, right_high))


def forward_spectra(columns, first_ref, ahead_ref, twist_ref):
    count = len(columns)
    high, low = halves(jnp.concatenate(columns, axis=1))
    first_high, first_low = halves(first_ref[...])
    mid = dot(jnp.concatenate([first_high, first_high], axis=1), jnp.concatenate([high, low], axis=0))
    mid = mid + dot(first_low, high)
    cos_t, sin_t = twist_ref[0], twist_ref[1]
    rows = []
    for u in range(count):
        real = mid[:side, u * side : (u + 1) * side]
        imag = mid[side:, u * side : (u + 1) * side]
        rows.append(
            jnp.concatenate([real * cos_t - imag * sin_t, real * sin_t + imag * cos_t], axis=1)
        )
    out = exact_dot(halves(jnp.concatenate(rows, axis=0)), halves(ahead_ref[...]))
    return [
        (out[u * side : (u + 1) * side, :side], out[u * side : (u + 1) * side, side:])
        for u in range(count)
    ]


def inverse_columns(spectra, back_ref, last_ref, twist_ref):
    count = len(spectra)
    stacked = jnp.concatenate([jnp.concatenate(pair, axis=1) for pair in spectra], axis=0)
    mid = exact_dot(halves(stacked), halves(back_ref[...]))
    cos_t, sin_t = twist_ref[0], twist_ref[1]
    cols = []
    for u in range(count):
        real = mid[u * side : (u + 1) * side, :side]
        imag = mid[u * side : (u + 1) * side, side:]
        cols.append(
            jnp.concatenate([real * cos_t + imag * sin_t, imag * cos_t - real * sin_t], axis=0)
        )
    return exact_dot(halves(last_ref[...]), halves(jnp.concatenate(cols, axis=1)))


def product(left, right):
    return (left[0] * right[0] - left[1] * right[1], left[0] * right[1] + left[1] * right[0])


def conj_product(left, right):
    return (left[0] * right[0] + left[1] * right[1], left[0] * right[1] - left[1] * right[0])


def slice_of(u):
    return slice(u * side, (u + 1) * side)


def first_kernel(key_hbm, value_hbm, filt_hbm, query_hbm, cot_hbm, gain_hbm, *refs):
    sent_ref, query_t_ref, cot_t_ref, scaled_t_ref = refs[:4]
    key_ref, value_ref, filt_ref, query_ref, cot_ref, gain_ref, sems = refs[4:]
    sources = (filt_hbm, key_hbm, value_hbm, query_hbm, cot_hbm, gain_hbm)
    targets = (filt_ref, key_ref, value_ref, query_ref, cot_ref, gain_ref)
    copies = [
        pltpu.make_async_copy(a, b, sems.at[i]) for i, (a, b) in enumerate(zip(sources, targets))
    ]
    for copy in copies:
        copy.start()
    halves_of = [slice(h * side, (h + 1) * side) for h in range(2)]
    copies[0].wait()
    for h, cols in enumerate(halves_of):
        sent_ref[:, h, :] = filt_ref[:, cols].T
    copies[1].wait()
    copies[2].wait()
    for h, cols in enumerate(halves_of):
        mixed = key_ref[:, cols].astype(jnp.float32) * value_ref[:, cols].astype(jnp.float32)
        sent_ref[:, 2 + h, :] = mixed.T
    for copy in copies[3:]:
        copy.wait()
    for h, cols in enumerate(halves_of):
        cot = cot_ref[:, cols].astype(jnp.float32)
        query_t_ref[cols, :] = query_ref[:, cols].astype(jnp.float32).T
        cot_t_ref[cols, :] = cot.T
        scaled_t_ref[cols, :] = (cot * gain_ref[:, cols]).T


def conv_kernel(got_ref, first_ref, ahead_ref, back_ref, last_ref, twist_ref, out_ref, spec_ref):
    columns = [got_ref[:, u, :] for u in range(4)]
    spectra = forward_spectra(columns, first_ref, ahead_ref, twist_ref)
    for u in range(4):
        spec_ref[u, 0] = spectra[u][0]
        spec_ref[u, 1] = spectra[u][1]
    both = [product(spectra[h], spectra[2 + h]) for h in range(2)]
    conv = inverse_columns(both, back_ref, last_ref, twist_ref)
    for h in range(2):
        out_ref[:, h, :] = conv[:, h * side : (h + 1) * side]


def row_sums_kernel(conv_ref, query_t_ref, scaled_t_ref, out_ref):
    squares = jnp.zeros((1, side), jnp.float32)
    dots = jnp.zeros((1, side), jnp.float32)
    for h in range(2):
        cols = slice(h * side, (h + 1) * side)
        gated = conv_ref[:, h, :] * query_t_ref[cols, :]
        squares = squares + jnp.sum(gated * gated, axis=0, keepdims=True)
        dots = dots + jnp.sum(scaled_t_ref[cols, :] * gated, axis=0, keepdims=True)
    out_ref[0:1, :] = squares
    out_ref[1:2, :] = dots


def row_scalars(sums_ref):
    squares = sums_ref[0, 0:1, :]
    dots = sums_ref[0, 1:2, :]
    for t in range(1, 4):
        squares = squares + sums_ref[t, 0:1, :]
        dots = dots + sums_ref[t, 1:2, :]
    inv_rms = lax.rsqrt(squares * (1.0 / channels) + norm_eps)
    return inv_rms, dots * (1.0 / channels)


def d_conv_kernel(conv_ref, query_t_ref, cot_t_ref, scaled_t_ref, sums_ref, out_ref):
    inv_rms, row_dot = row_scalars(sums_ref)
    pull = inv_rms * inv_rms * inv_rms * row_dot
    parts = []
    for h in range(2):
        cols = slice(h * side, (h + 1) * side)
        query = query_t_ref[cols, :]
        cot = cot_t_ref[cols, :]
        gated = conv_ref[:, h, :] * query
        scaled = scaled_t_ref[cols, :]
        out_ref[:, 0, slice_of(h)] = (inv_rms * scaled - gated * pull) * query
        part = jnp.sum(cot * gated * inv_rms, axis=1, keepdims=True)
        parts.append(jnp.broadcast_to(part, (side, side)).T)
    number = lax.broadcasted_iota(jnp.int32, (side, side), 0)
    out_ref[:, 0, slice_of(2)] = jnp.where((number & 2) == 0, parts[0], parts[1])


def row_outputs_kernel(
    conv_ref,
    query_t_ref,
    scaled_t_ref,
    sums_ref,
    gain_ref,
    got_ref,
    output_ref,
    grad_query_ref,
    gain_half_ref,
):
    inv_rms, row_dot = row_scalars(sums_ref)
    pull = inv_rms * inv_rms * inv_rms * row_dot
    for h in range(2):
        cols = slice(h * side, (h + 1) * side)
        conv = conv_ref[:, h, :]
        gated = conv * query_t_ref[cols, :]
        scaled = scaled_t_ref[cols, :]
        normed = (gated * inv_rms).T
        output_ref[:, cols] = (normed * gain_ref[:, cols]).astype(jnp.bfloat16)
        grad = (inv_rms * scaled - gated * pull) * conv
        grad_query_ref[:, cols] = grad.T.astype(jnp.bfloat16)
    gain_half_ref[...] = jnp.sum(got_ref[:, 0, slice_of(2)], axis=0, keepdims=True)


def corr_kernel(
    got_ref, spec_ref, first_ref, ahead_ref, back_ref, last_ref, twist_ref, out_ref
):
    columns = [got_ref[:, 0, slice_of(h)] for h in range(2)]
    spectra = forward_spectra(columns, first_ref, ahead_ref, twist_ref)
    pairs = [
        conj_product((spec_ref[u, 0], spec_ref[u, 1]), spectra[u % 2]) for u in range(4)
    ]
    result = inverse_columns(pairs, back_ref, last_ref, twist_ref)
    for u in range(4):
        out_ref[:, u, :] = result[:, u * side : (u + 1) * side]


def last_outputs_kernel(
    got_ref, key_ref, value_ref, grad_key_ref, grad_value_ref, grad_filter_ref
):
    for h in range(2):
        cols = slice(h * side, (h + 1) * side)
        d_mixed = got_ref[:, h, :].T
        value = value_ref[:, cols].astype(jnp.float32)
        key = key_ref[:, cols].astype(jnp.float32)
        grad_key_ref[:, cols] = (d_mixed * value).astype(jnp.bfloat16)
        grad_value_ref[:, cols] = (d_mixed * key).astype(jnp.bfloat16)
        grad_filter_ref[:, cols] = got_ref[:, 2 + h, :].T


def call(kernel, outs, *operands, **options):
    moved = sum(math.prod(o.shape) * o.dtype.itemsize for o in operands)
    moved += sum(math.prod(o.shape) * o.dtype.itemsize for o in outs)
    result = pl.pallas_call(
        kernel,
        out_shape=outs,
        compiler_params=pltpu.CompilerParams(vmem_limit_bytes=vmem_bytes),
        cost_estimate=pl.CostEstimate(flops=0, bytes_accessed=moved, transcendentals=0),
        **options,
    )(*operands)
    return result


def f32(*shape):
    return jax.ShapeDtypeStruct(shape, jnp.float32)


def bf16(*shape):
    return jax.ShapeDtypeStruct(shape, jnp.bfloat16)


def swap(sent):
    got = lax.all_to_all(
        sent,
        "ctx",
        split_axis=0,
        concat_axis=0,
        axis_index_groups=[swap_order()],
        tiled=True,
    )
    return got


def per_device(gate_query, key_proj, value_proj, long_filter, out_gain, cotangent):
    *tables, twist = (jnp.asarray(t) for t in make_tables())
    wide = 2 * side
    gain = out_gain.reshape(1, wide)

    in_hbm = pl.BlockSpec(memory_space=pltpu.HBM)
    inputs = (key_proj, value_proj, long_filter, gate_query, cotangent, gain)
    sent, query_t, cot_t, scaled_t = call(
        first_kernel,
        (f32(side, 4, side),) + (f32(wide, side),) * 3,
        *(pltpu.with_memory_space_constraint(x, pltpu.HBM) for x in inputs),
        in_specs=[in_hbm] * 6,
        scratch_shapes=[
            pltpu.VMEM((side, wide), jnp.bfloat16),
            pltpu.VMEM((side, wide), jnp.bfloat16),
            pltpu.VMEM((side, wide), jnp.float32),
            pltpu.VMEM((side, wide), jnp.bfloat16),
            pltpu.VMEM((side, wide), jnp.bfloat16),
            pltpu.VMEM((1, wide), jnp.float32),
            pltpu.SemaphoreType.DMA((6,)),
        ],
    )
    got = swap(sent)
    sent, spectra = call(
        conv_kernel, (f32(side, 2, side), f32(4, 2, side, side)), got, *tables, twist
    )
    conv_t = swap(sent)
    (sums,) = call(row_sums_kernel, (f32(2, side),), conv_t, query_t, scaled_t)
    sums = lax.all_gather(sums, "tp")
    (sent,) = call(d_conv_kernel, (f32(side, 1, 3 * side),), conv_t, query_t, cot_t, scaled_t, sums)
    got = swap(sent)
    output, grad_query, gain_half = call(
        row_outputs_kernel,
        (bf16(side, wide), bf16(side, wide), f32(1, side)),
        conv_t,
        query_t,
        scaled_t,
        sums,
        gain,
        got,
    )
    other_half = lax.ppermute(gain_half, "ctx", [(i, i ^ 1) for i in range(side)])
    odd = (lax.axis_index("ctx") & 1) == 1
    grad_gain = jnp.concatenate(
        [jnp.where(odd, other_half, gain_half), jnp.where(odd, gain_half, other_half)], axis=1
    )
    (sent,) = call(
        corr_kernel,
        (f32(side, 4, side),),
        got,
        spectra,
        *tables,
        twist,
    )
    got = swap(sent)
    grad_key, grad_value, grad_filter = call(
        last_outputs_kernel,
        (bf16(side, wide), bf16(side, wide), f32(side, wide)),
        got,
        key_proj,
        value_proj,
    )
    return (output, grad_query, grad_key, grad_value, grad_filter, grad_gain.reshape(wide))


def solution(mesh):
    both = P("ctx", "tp")
    return jax.shard_map(
        per_device,
        mesh=mesh,
        in_specs=(both, both, both, both, P("tp"), both),
        out_specs=(both, both, both, both, both, P("tp")),
        check_vma=False,
    )
```

```python
import math

import jax
import jax.numpy as jnp
import numpy as np
from jax import lax
from jax.experimental import pallas as pl
from jax.experimental.pallas import tpu as pltpu
from jax.sharding import PartitionSpec as P

norm_eps = 1e-06
side = 128
length = side * side
channels = 1024
ctx_sizes = (2, 16, 4)
vmem_bytes = 40 * 1024 * 1024


def swap_order():
    grid = np.arange(side).reshape(ctx_sizes).transpose(1, 2, 0)
    return np.roll(grid, (8, 2, 1), axis=(0, 1, 2)).reshape(-1).tolist()


def make_tables():
    block = np.array(swap_order())
    idx = np.arange(side)
    ang_a = 2.0 * math.pi * ((idx[:, None] + 0.25) * block[None, :] / side)
    cos_a, sin_a = np.cos(ang_a), np.sin(ang_a)
    first = np.concatenate([cos_a, sin_a], axis=0)
    scale = 1.0 / length / math.sqrt(length)
    last = np.concatenate([cos_a.T, sin_a.T], axis=1) * scale
    ang_t = 2.0 * math.pi * ((idx[:, None] + 0.25) * idx[None, :] / length)
    twist = np.stack([np.cos(ang_t), np.sin(ang_t)]).astype(np.float32)
    ang_b = 2.0 * math.pi * (idx[:, None] * idx[None, :] % side) / side
    cos_b, sin_b = np.cos(ang_b), np.sin(ang_b)
    ahead = np.block([[cos_b, sin_b], [-sin_b, cos_b]])
    back = np.block([[cos_b, -sin_b], [sin_b, cos_b]])
    return tuple(t.astype(np.float32) for t in (first, ahead, back, last)) + (twist,)


def exact_dot(left, right):
    return jnp.dot(
        left, right, precision=lax.Precision.HIGHEST, preferred_element_type=jnp.float32
    )


def forward_spectra(columns, first_ref, ahead_ref, twist_ref):
    count = len(columns)
    mid = exact_dot(first_ref[...], jnp.concatenate(columns, axis=1))
    cos_t, sin_t = twist_ref[0], twist_ref[1]
    rows = []
    for u in range(count):
        real = mid[:side, u * side : (u + 1) * side]
        imag = mid[side:, u * side : (u + 1) * side]
        rows.append(
            jnp.concatenate([real * cos_t - imag * sin_t, real * sin_t + imag * cos_t], axis=1)
        )
    out = exact_dot(jnp.concatenate(rows, axis=0), ahead_ref[...])
    return [
        (out[u * side : (u + 1) * side, :side], out[u * side : (u + 1) * side, side:])
        for u in range(count)
    ]


def inverse_columns(spectra, back_ref, last_ref, twist_ref):
    count = len(spectra)
    stacked = jnp.concatenate([jnp.concatenate(pair, axis=1) for pair in spectra], axis=0)
    mid = exact_dot(stacked, back_ref[...])
    cos_t, sin_t = twist_ref[0], twist_ref[1]
    cols = []
    for u in range(count):
        real = mid[u * side : (u + 1) * side, :side]
        imag = mid[u * side : (u + 1) * side, side:]
        cols.append(
            jnp.concatenate([real * cos_t + imag * sin_t, imag * cos_t - real * sin_t], axis=0)
        )
    return exact_dot(last_ref[...], jnp.concatenate(cols, axis=1))


def product(left, right):
    return (left[0] * right[0] - left[1] * right[1], left[0] * right[1] + left[1] * right[0])


def conj_product(left, right):
    return (left[0] * right[0] + left[1] * right[1], left[0] * right[1] - left[1] * right[0])


def slice_of(u):
    return slice(u * side, (u + 1) * side)


def first_kernel(key_hbm, value_hbm, filt_hbm, query_hbm, cot_hbm, gain_hbm, *refs):
    sent_ref, query_t_ref, cot_t_ref, scaled_t_ref = refs[:4]
    key_ref, value_ref, filt_ref, query_ref, cot_ref, gain_ref, sems = refs[4:]
    sources = (filt_hbm, key_hbm, value_hbm, query_hbm, cot_hbm, gain_hbm)
    targets = (filt_ref, key_ref, value_ref, query_ref, cot_ref, gain_ref)
    copies = [
        pltpu.make_async_copy(a, b, sems.at[i]) for i, (a, b) in enumerate(zip(sources, targets))
    ]
    for copy in copies:
        copy.start()
    halves_of = [slice(h * side, (h + 1) * side) for h in range(2)]
    copies[0].wait()
    for h, cols in enumerate(halves_of):
        sent_ref[:, h, :] = filt_ref[:, cols].T
    copies[1].wait()
    copies[2].wait()
    for h, cols in enumerate(halves_of):
        mixed = key_ref[:, cols].astype(jnp.float32) * value_ref[:, cols].astype(jnp.float32)
        sent_ref[:, 2 + h, :] = mixed.T
    for copy in copies[3:]:
        copy.wait()
    for h, cols in enumerate(halves_of):
        cot = cot_ref[:, cols].astype(jnp.float32)
        query_t_ref[cols, :] = query_ref[:, cols].astype(jnp.float32).T
        cot_t_ref[cols, :] = cot.T
        scaled_t_ref[cols, :] = (cot * gain_ref[:, cols]).T


def conv_kernel(got_ref, first_ref, ahead_ref, back_ref, last_ref, twist_ref, out_ref, spec_ref):
    columns = [got_ref[:, u, :] for u in range(4)]
    spectra = forward_spectra(columns, first_ref, ahead_ref, twist_ref)
    for u in range(4):
        spec_ref[u, 0] = spectra[u][0]
        spec_ref[u, 1] = spectra[u][1]
    both = [product(spectra[h], spectra[2 + h]) for h in range(2)]
    conv = inverse_columns(both, back_ref, last_ref, twist_ref)
    for h in range(2):
        out_ref[:, h, :] = conv[:, h * side : (h + 1) * side]


def row_sums_kernel(conv_ref, query_t_ref, scaled_t_ref, out_ref):
    squares = jnp.zeros((1, side), jnp.float32)
    dots = jnp.zeros((1, side), jnp.float32)
    for h in range(2):
        cols = slice(h * side, (h + 1) * side)
        gated = conv_ref[:, h, :] * query_t_ref[cols, :]
        squares = squares + jnp.sum(gated * gated, axis=0, keepdims=True)
        dots = dots + jnp.sum(scaled_t_ref[cols, :] * gated, axis=0, keepdims=True)
    out_ref[0:1, :] = squares
    out_ref[1:2, :] = dots


def row_scalars(sums_ref):
    squares = sums_ref[0, 0:1, :]
    dots = sums_ref[0, 1:2, :]
    for t in range(1, 4):
        squares = squares + sums_ref[t, 0:1, :]
        dots = dots + sums_ref[t, 1:2, :]
    inv_rms = lax.rsqrt(squares * (1.0 / channels) + norm_eps)
    return inv_rms, dots * (1.0 / channels)


def d_conv_kernel(conv_ref, query_t_ref, cot_t_ref, scaled_t_ref, sums_ref, out_ref):
    inv_rms, row_dot = row_scalars(sums_ref)
    pull = inv_rms * inv_rms * inv_rms * row_dot
    parts = []
    for h in range(2):
        cols = slice(h * side, (h + 1) * side)
        query = query_t_ref[cols, :]
        cot = cot_t_ref[cols, :]
        gated = conv_ref[:, h, :] * query
        scaled = scaled_t_ref[cols, :]
        out_ref[:, 0, slice_of(h)] = (inv_rms * scaled - gated * pull) * query
        part = jnp.sum(cot * gated * inv_rms, axis=1, keepdims=True)
        parts.append(jnp.broadcast_to(part, (side, side)).T)
    number = lax.broadcasted_iota(jnp.int32, (side, side), 0)
    out_ref[:, 0, slice_of(2)] = jnp.where((number & 2) == 0, parts[0], parts[1])


def row_outputs_kernel(
    conv_ref,
    query_t_ref,
    scaled_t_ref,
    sums_ref,
    gain_ref,
    got_ref,
    output_ref,
    grad_query_ref,
    gain_half_ref,
):
    inv_rms, row_dot = row_scalars(sums_ref)
    pull = inv_rms * inv_rms * inv_rms * row_dot
    for h in range(2):
        cols = slice(h * side, (h + 1) * side)
        conv = conv_ref[:, h, :]
        gated = conv * query_t_ref[cols, :]
        scaled = scaled_t_ref[cols, :]
        normed = (gated * inv_rms).T
        output_ref[:, cols] = (normed * gain_ref[:, cols]).astype(jnp.bfloat16)
        grad = (inv_rms * scaled - gated * pull) * conv
        grad_query_ref[:, cols] = grad.T.astype(jnp.bfloat16)
    gain_half_ref[...] = jnp.sum(got_ref[:, 0, slice_of(2)], axis=0, keepdims=True)


def corr_kernel(
    got_ref, spec_ref, first_ref, ahead_ref, back_ref, last_ref, twist_ref, out_ref
):
    columns = [got_ref[:, 0, slice_of(h)] for h in range(2)]
    spectra = forward_spectra(columns, first_ref, ahead_ref, twist_ref)
    pairs = [
        conj_product((spec_ref[u, 0], spec_ref[u, 1]), spectra[u % 2]) for u in range(4)
    ]
    result = inverse_columns(pairs, back_ref, last_ref, twist_ref)
    for u in range(4):
        out_ref[:, u, :] = result[:, u * side : (u + 1) * side]


def last_outputs_kernel(
    got_ref, key_ref, value_ref, grad_key_ref, grad_value_ref, grad_filter_ref
):
    for h in range(2):
        cols = slice(h * side, (h + 1) * side)
        d_mixed = got_ref[:, h, :].T
        value = value_ref[:, cols].astype(jnp.float32)
        key = key_ref[:, cols].astype(jnp.float32)
        grad_key_ref[:, cols] = (d_mixed * value).astype(jnp.bfloat16)
        grad_value_ref[:, cols] = (d_mixed * key).astype(jnp.bfloat16)
        grad_filter_ref[:, cols] = got_ref[:, 2 + h, :].T


def call(kernel, outs, *operands, **options):
    moved = sum(math.prod(o.shape) * o.dtype.itemsize for o in operands)
    moved += sum(math.prod(o.shape) * o.dtype.itemsize for o in outs)
    result = pl.pallas_call(
        kernel,
        out_shape=outs,
        compiler_params=pltpu.CompilerParams(vmem_limit_bytes=vmem_bytes),
        cost_estimate=pl.CostEstimate(flops=0, bytes_accessed=moved, transcendentals=0),
        **options,
    )(*operands)
    return result


def f32(*shape):
    return jax.ShapeDtypeStruct(shape, jnp.float32)


def bf16(*shape):
    return jax.ShapeDtypeStruct(shape, jnp.bfloat16)


def swap(sent):
    got = lax.all_to_all(
        sent,
        "ctx",
        split_axis=0,
        concat_axis=0,
        axis_index_groups=[swap_order()],
        tiled=True,
    )
    return got


def per_device(gate_query, key_proj, value_proj, long_filter, out_gain, cotangent):
    *tables, twist = (jnp.asarray(t) for t in make_tables())
    wide = 2 * side
    gain = out_gain.reshape(1, wide)

    in_hbm = pl.BlockSpec(memory_space=pltpu.HBM)
    inputs = (key_proj, value_proj, long_filter, gate_query, cotangent, gain)
    sent, query_t, cot_t, scaled_t = call(
        first_kernel,
        (f32(side, 4, side),) + (f32(wide, side),) * 3,
        *(pltpu.with_memory_space_constraint(x, pltpu.HBM) for x in inputs),
        in_specs=[in_hbm] * 6,
        scratch_shapes=[
            pltpu.VMEM((side, wide), jnp.bfloat16),
            pltpu.VMEM((side, wide), jnp.bfloat16),
            pltpu.VMEM((side, wide), jnp.float32),
            pltpu.VMEM((side, wide), jnp.bfloat16),
            pltpu.VMEM((side, wide), jnp.bfloat16),
            pltpu.VMEM((1, wide), jnp.float32),
            pltpu.SemaphoreType.DMA((6,)),
        ],
    )
    got = swap(sent)
    sent, spectra = call(
        conv_kernel, (f32(side, 2, side), f32(4, 2, side, side)), got, *tables, twist
    )
    conv_t = swap(sent)
    (sums,) = call(row_sums_kernel, (f32(2, side),), conv_t, query_t, scaled_t)
    sums = lax.all_gather(sums, "tp")
    (sent,) = call(d_conv_kernel, (f32(side, 1, 3 * side),), conv_t, query_t, cot_t, scaled_t, sums)
    got = swap(sent)
    output, grad_query, gain_half = call(
        row_outputs_kernel,
        (bf16(side, wide), bf16(side, wide), f32(1, side)),
        conv_t,
        query_t,
        scaled_t,
        sums,
        gain,
        got,
    )
    other_half = lax.ppermute(gain_half, "ctx", [(i, i ^ 1) for i in range(side)])
    odd = (lax.axis_index("ctx") & 1) == 1
    grad_gain = jnp.concatenate(
        [jnp.where(odd, other_half, gain_half), jnp.where(odd, gain_half, other_half)], axis=1
    )
    (sent,) = call(
        corr_kernel,
        (f32(side, 4, side),),
        got,
        spectra,
        *tables,
        twist,
    )
    got = swap(sent)
    grad_key, grad_value, grad_filter = call(
        last_outputs_kernel,
        (bf16(side, wide), bf16(side, wide), f32(side, wide)),
        got,
        key_proj,
        value_proj,
    )
    return (output, grad_query, grad_key, grad_value, grad_filter, grad_gain.reshape(wide))


def solution(mesh):
    both = P("ctx", "tp")
    return jax.shard_map(
        per_device,
        mesh=mesh,
        in_specs=(both, both, both, both, P("tp"), both),
        out_specs=(both, both, both, both, both, P("tp")),
        check_vma=False,
    )
```

```python
import math

import jax
import jax.numpy as jnp
import numpy as np
from jax import lax
from jax.experimental import pallas as pl
from jax.experimental.pallas import tpu as pltpu
from jax.sharding import PartitionSpec as P

norm_eps = 1e-06
side = 128
length = side * side
channels = 1024
ctx_sizes = (2, 16, 4)
vmem_bytes = 40 * 1024 * 1024


def swap_order():
    grid = np.arange(side).reshape(ctx_sizes).transpose(1, 2, 0)
    return np.roll(grid, (8, 2, 1), axis=(0, 1, 2)).reshape(-1).tolist()


def make_tables():
    block = np.array(swap_order())
    idx = np.arange(side)
    ang_a = 2.0 * math.pi * ((idx[:, None] + 0.25) * block[None, :] / side)
    cos_a, sin_a = np.cos(ang_a), np.sin(ang_a)
    first = np.concatenate([cos_a, sin_a], axis=0)
    scale = 1.0 / length / math.sqrt(length)
    last = np.concatenate([cos_a.T, sin_a.T], axis=1) * scale
    ang_t = 2.0 * math.pi * ((idx[:, None] + 0.25) * idx[None, :] / length)
    twist = np.stack([np.cos(ang_t), np.sin(ang_t)]).astype(np.float32)
    ang_b = 2.0 * math.pi * (idx[:, None] * idx[None, :] % side) / side
    cos_b, sin_b = np.cos(ang_b), np.sin(ang_b)
    ahead = np.block([[cos_b, sin_b], [-sin_b, cos_b]])
    back = np.block([[cos_b, -sin_b], [sin_b, cos_b]])
    return tuple(t.astype(np.float32) for t in (first, ahead, back, last)) + (twist,)


def exact_dot(left, right):
    return jnp.dot(
        left, right, precision=lax.Precision.HIGHEST, preferred_element_type=jnp.float32
    )


def forward_spectra(columns, first_ref, ahead_ref, twist_ref):
    count = len(columns)
    mid = exact_dot(first_ref[...], jnp.concatenate(columns, axis=1))
    cos_t, sin_t = twist_ref[0], twist_ref[1]
    rows = []
    for u in range(count):
        real = mid[:side, u * side : (u + 1) * side]
        imag = mid[side:, u * side : (u + 1) * side]
        rows.append(
            jnp.concatenate([real * cos_t - imag * sin_t, real * sin_t + imag * cos_t], axis=1)
        )
    out = exact_dot(jnp.concatenate(rows, axis=0), ahead_ref[...])
    return [
        (out[u * side : (u + 1) * side, :side], out[u * side : (u + 1) * side, side:])
        for u in range(count)
    ]


def inverse_columns(spectra, back_ref, last_ref, twist_ref):
    count = len(spectra)
    stacked = jnp.concatenate([jnp.concatenate(pair, axis=1) for pair in spectra], axis=0)
    mid = exact_dot(stacked, back_ref[...])
    cos_t, sin_t = twist_ref[0], twist_ref[1]
    cols = []
    for u in range(count):
        real = mid[u * side : (u + 1) * side, :side]
        imag = mid[u * side : (u + 1) * side, side:]
        cols.append(
            jnp.concatenate([real * cos_t + imag * sin_t, imag * cos_t - real * sin_t], axis=0)
        )
    return exact_dot(last_ref[...], jnp.concatenate(cols, axis=1))


def product(left, right):
    return (left[0] * right[0] - left[1] * right[1], left[0] * right[1] + left[1] * right[0])


def conj_product(left, right):
    return (left[0] * right[0] + left[1] * right[1], left[0] * right[1] - left[1] * right[0])


def every(start, stride):
    return pl.ds(start, side, stride=stride)


def first_kernel(key_hbm, value_hbm, filt_hbm, query_hbm, cot_hbm, gain_hbm, *refs):
    sent_ref, query_t_ref, cot_t_ref, scaled_t_ref = refs[:4]
    key_ref, value_ref, filt_ref, query_ref, cot_ref, gain_ref, sems = refs[4:]
    sources = (filt_hbm, key_hbm, value_hbm, query_hbm, cot_hbm, gain_hbm)
    targets = (filt_ref, key_ref, value_ref, query_ref, cot_ref, gain_ref)
    copies = [
        pltpu.make_async_copy(a, b, sems.at[i]) for i, (a, b) in enumerate(zip(sources, targets))
    ]
    for copy in copies:
        copy.start()
    halves_of = [slice(h * side, (h + 1) * side) for h in range(2)]
    copies[0].wait()
    for h, cols in enumerate(halves_of):
        sent_ref[every(h, 4), :] = filt_ref[:, cols].T
    copies[1].wait()
    copies[2].wait()
    for h, cols in enumerate(halves_of):
        mixed = key_ref[:, cols].astype(jnp.float32) * value_ref[:, cols].astype(jnp.float32)
        sent_ref[every(2 + h, 4), :] = mixed.T
    for copy in copies[3:]:
        copy.wait()
    for h, cols in enumerate(halves_of):
        cot = cot_ref[:, cols].astype(jnp.float32)
        query_t_ref[cols, :] = query_ref[:, cols].astype(jnp.float32).T
        cot_t_ref[cols, :] = cot.T
        scaled_t_ref[cols, :] = (cot * gain_ref[:, cols]).T


def conv_kernel(got_ref, first_ref, ahead_ref, back_ref, last_ref, twist_ref, out_ref, spec_ref):
    columns = [got_ref[every(u, 4), :] for u in range(4)]
    spectra = forward_spectra(columns, first_ref, ahead_ref, twist_ref)
    for u in range(4):
        spec_ref[u, 0] = spectra[u][0]
        spec_ref[u, 1] = spectra[u][1]
    both = [product(spectra[h], spectra[2 + h]) for h in range(2)]
    conv = inverse_columns(both, back_ref, last_ref, twist_ref)
    for h in range(2):
        out_ref[every(h, 2), :] = conv[:, h * side : (h + 1) * side]


def row_sums_kernel(conv_ref, query_t_ref, scaled_t_ref, out_ref):
    squares = jnp.zeros((1, side), jnp.float32)
    dots = jnp.zeros((1, side), jnp.float32)
    for h in range(2):
        cols = slice(h * side, (h + 1) * side)
        gated = conv_ref[every(h, 2), :] * query_t_ref[cols, :]
        squares = squares + jnp.sum(gated * gated, axis=0, keepdims=True)
        dots = dots + jnp.sum(scaled_t_ref[cols, :] * gated, axis=0, keepdims=True)
    out_ref[0:1, :] = squares
    out_ref[1:2, :] = dots


def row_scalars(sums_ref):
    squares = sums_ref[0, 0:1, :]
    dots = sums_ref[0, 1:2, :]
    for t in range(1, 4):
        squares = squares + sums_ref[t, 0:1, :]
        dots = dots + sums_ref[t, 1:2, :]
    inv_rms = lax.rsqrt(squares * (1.0 / channels) + norm_eps)
    return inv_rms, dots * (1.0 / channels)


def d_conv_kernel(conv_ref, query_t_ref, cot_t_ref, scaled_t_ref, sums_ref, out_ref):
    inv_rms, row_dot = row_scalars(sums_ref)
    pull = inv_rms * inv_rms * inv_rms * row_dot
    parts = []
    for h in range(2):
        cols = slice(h * side, (h + 1) * side)
        query = query_t_ref[cols, :]
        cot = cot_t_ref[cols, :]
        gated = conv_ref[every(h, 2), :] * query
        scaled = scaled_t_ref[cols, :]
        out_ref[every(h, 3), :] = (inv_rms * scaled - gated * pull) * query
        part = jnp.sum(cot * gated * inv_rms, axis=1, keepdims=True)
        parts.append(jnp.broadcast_to(part, (side, side)).T)
    number = lax.broadcasted_iota(jnp.int32, (side, side), 0)
    out_ref[every(2, 3), :] = jnp.where((number & 2) == 0, parts[0], parts[1])


def row_outputs_kernel(
    conv_ref,
    query_t_ref,
    scaled_t_ref,
    sums_ref,
    gain_ref,
    got_ref,
    output_ref,
    grad_query_ref,
    gain_half_ref,
):
    inv_rms, row_dot = row_scalars(sums_ref)
    pull = inv_rms * inv_rms * inv_rms * row_dot
    for h in range(2):
        cols = slice(h * side, (h + 1) * side)
        conv = conv_ref[every(h, 2), :]
        gated = conv * query_t_ref[cols, :]
        scaled = scaled_t_ref[cols, :]
        normed = (gated * inv_rms).T
        output_ref[:, cols] = (normed * gain_ref[:, cols]).astype(jnp.bfloat16)
        grad = (inv_rms * scaled - gated * pull) * conv
        grad_query_ref[:, cols] = grad.T.astype(jnp.bfloat16)
    gain_half_ref[...] = jnp.sum(got_ref[every(2, 3), :], axis=0, keepdims=True)


def corr_kernel(
    got_ref, spec_ref, first_ref, ahead_ref, back_ref, last_ref, twist_ref, out_ref
):
    columns = [got_ref[every(h, 3), :] for h in range(2)]
    spectra = forward_spectra(columns, first_ref, ahead_ref, twist_ref)
    pairs = [
        conj_product((spec_ref[u, 0], spec_ref[u, 1]), spectra[u % 2]) for u in range(4)
    ]
    result = inverse_columns(pairs, back_ref, last_ref, twist_ref)
    for u in range(4):
        out_ref[every(u, 4), :] = result[:, u * side : (u + 1) * side]


def last_outputs_kernel(
    got_ref, key_ref, value_ref, grad_key_ref, grad_value_ref, grad_filter_ref
):
    for h in range(2):
        cols = slice(h * side, (h + 1) * side)
        d_mixed = got_ref[every(h, 4), :].T
        value = value_ref[:, cols].astype(jnp.float32)
        key = key_ref[:, cols].astype(jnp.float32)
        grad_key_ref[:, cols] = (d_mixed * value).astype(jnp.bfloat16)
        grad_value_ref[:, cols] = (d_mixed * key).astype(jnp.bfloat16)
        grad_filter_ref[:, cols] = got_ref[every(2 + h, 4), :].T


def call(kernel, outs, *operands, **options):
    moved = sum(math.prod(o.shape) * o.dtype.itemsize for o in operands)
    moved += sum(math.prod(o.shape) * o.dtype.itemsize for o in outs)
    result = pl.pallas_call(
        kernel,
        out_shape=outs,
        compiler_params=pltpu.CompilerParams(vmem_limit_bytes=vmem_bytes),
        cost_estimate=pl.CostEstimate(flops=0, bytes_accessed=moved, transcendentals=0),
        **options,
    )(*operands)
    return result


def f32(*shape):
    return jax.ShapeDtypeStruct(shape, jnp.float32)


def bf16(*shape):
    return jax.ShapeDtypeStruct(shape, jnp.bfloat16)


def swap(sent, rows):
    shape = (side, 1, rows * side) if rows == 3 else (side, rows, side)
    got = lax.all_to_all(
        sent.reshape(shape),
        "ctx",
        split_axis=0,
        concat_axis=0,
        axis_index_groups=[swap_order()],
        tiled=True,
    )
    return got.reshape(side * rows, side)


def per_device(gate_query, key_proj, value_proj, long_filter, out_gain, cotangent):
    *tables, twist = (jnp.asarray(t) for t in make_tables())
    wide = 2 * side
    gain = out_gain.reshape(1, wide)

    in_hbm = pl.BlockSpec(memory_space=pltpu.HBM)
    inputs = (key_proj, value_proj, long_filter, gate_query, cotangent, gain)
    sent, query_t, cot_t, scaled_t = call(
        first_kernel,
        (f32(4 * side, side),) + (f32(wide, side),) * 3,
        *(pltpu.with_memory_space_constraint(x, pltpu.HBM) for x in inputs),
        in_specs=[in_hbm] * 6,
        scratch_shapes=[
            pltpu.VMEM((side, wide), jnp.bfloat16),
            pltpu.VMEM((side, wide), jnp.bfloat16),
            pltpu.VMEM((side, wide), jnp.float32),
            pltpu.VMEM((side, wide), jnp.bfloat16),
            pltpu.VMEM((side, wide), jnp.bfloat16),
            pltpu.VMEM((1, wide), jnp.float32),
            pltpu.SemaphoreType.DMA((6,)),
        ],
    )
    got = swap(sent, 4)
    sent, spectra = call(
        conv_kernel, (f32(wide, side), f32(4, 2, side, side)), got, *tables, twist
    )
    conv_t = swap(sent, 2)
    (sums,) = call(row_sums_kernel, (f32(2, side),), conv_t, query_t, scaled_t)
    sums = lax.all_gather(sums, "tp")
    (sent,) = call(d_conv_kernel, (f32(3 * side, side),), conv_t, query_t, cot_t, scaled_t, sums)
    got = swap(sent, 3)
    output, grad_query, gain_half = call(
        row_outputs_kernel,
        (bf16(side, wide), bf16(side, wide), f32(1, side)),
        conv_t,
        query_t,
        scaled_t,
        sums,
        gain,
        got,
    )
    other_half = lax.ppermute(gain_half, "ctx", [(i, i ^ 1) for i in range(side)])
    odd = (lax.axis_index("ctx") & 1) == 1
    grad_gain = jnp.concatenate(
        [jnp.where(odd, other_half, gain_half), jnp.where(odd, gain_half, other_half)], axis=1
    )
    (sent,) = call(
        corr_kernel,
        (f32(4 * side, side),),
        got,
        spectra,
        *tables,
        twist,
    )
    got = swap(sent, 4)
    grad_key, grad_value, grad_filter = call(
        last_outputs_kernel,
        (bf16(side, wide), bf16(side, wide), f32(side, wide)),
        got,
        key_proj,
        value_proj,
    )
    return (output, grad_query, grad_key, grad_value, grad_filter, grad_gain.reshape(wide))


def solution(mesh):
    both = P("ctx", "tp")
    return jax.shard_map(
        per_device,
        mesh=mesh,
        in_specs=(both, both, both, both, P("tp"), both),
        out_specs=(both, both, both, both, both, P("tp")),
        check_vma=False,
    )
```

```python
import math

import jax
import jax.numpy as jnp
import numpy as np
from jax import lax
from jax.experimental import pallas as pl
from jax.experimental.pallas import tpu as pltpu
from jax.sharding import PartitionSpec as P

norm_eps = 1e-06
side = 128
length = side * side
channels = 1024
ctx_sizes = (2, 16, 4)
vmem_bytes = 40 * 1024 * 1024


def swap_order():
    grid = np.arange(side).reshape(ctx_sizes).transpose(1, 2, 0)
    return np.roll(grid, (8, 2, 1), axis=(0, 1, 2)).reshape(-1).tolist()


def make_tables():
    block = np.array(swap_order())
    idx = np.arange(side)
    ang_a = 2.0 * math.pi * ((idx[:, None] + 0.25) * block[None, :] / side)
    cos_a, sin_a = np.cos(ang_a), np.sin(ang_a)
    first = np.concatenate([cos_a, sin_a], axis=0)
    scale = 1.0 / length / math.sqrt(length)
    last = np.concatenate([cos_a.T, sin_a.T], axis=1) * scale
    ang_t = 2.0 * math.pi * ((idx[:, None] + 0.25) * idx[None, :] / length)
    twist = np.stack([np.cos(ang_t), np.sin(ang_t)]).astype(np.float32)
    ang_b = 2.0 * math.pi * (idx[:, None] * idx[None, :] % side) / side
    cos_b, sin_b = np.cos(ang_b), np.sin(ang_b)
    ahead = np.block([[cos_b, sin_b], [-sin_b, cos_b]])
    back = np.block([[cos_b, -sin_b], [sin_b, cos_b]])
    return tuple(t.astype(np.float32) for t in (first, ahead, back, last)) + (twist,)


def halves(value):
    high = value.astype(jnp.bfloat16)
    low = (value - high.astype(jnp.float32)).astype(jnp.bfloat16)
    return high, low


def dot(left, right):
    return jnp.dot(left, right, preferred_element_type=jnp.float32)


def exact_dot(left, right):
    (left_high, left_low), (right_high, right_low) = left, right
    return dot(left_high, right_high) + (dot(left_high, right_low) + dot(left_low, right_high))


def forward_spectra(columns, first_ref, ahead_ref, twist_ref):
    count = len(columns)
    high, low = halves(jnp.concatenate(columns, axis=1))
    first_high, first_low = halves(first_ref[...])
    mid = dot(jnp.concatenate([first_high, first_high], axis=1), jnp.concatenate([high, low], axis=0))
    mid = mid + dot(first_low, high)
    cos_t, sin_t = twist_ref[0], twist_ref[1]
    rows = []
    for u in range(count):
        real = mid[:side, u * side : (u + 1) * side]
        imag = mid[side:, u * side : (u + 1) * side]
        rows.append(
            jnp.concatenate([real * cos_t - imag * sin_t, real * sin_t + imag * cos_t], axis=1)
        )
    out = exact_dot(halves(jnp.concatenate(rows, axis=0)), halves(ahead_ref[...]))
    return [
        (out[u * side : (u + 1) * side, :side], out[u * side : (u + 1) * side, side:])
        for u in range(count)
    ]


def inverse_columns(spectra, back_ref, last_ref, twist_ref):
    count = len(spectra)
    stacked = jnp.concatenate([jnp.concatenate(pair, axis=1) for pair in spectra], axis=0)
    mid = exact_dot(halves(stacked), halves(back_ref[...]))
    cos_t, sin_t = twist_ref[0], twist_ref[1]
    cols = []
    for u in range(count):
        real = mid[u * side : (u + 1) * side, :side]
        imag = mid[u * side : (u + 1) * side, side:]
        cols.append(
            jnp.concatenate([real * cos_t + imag * sin_t, imag * cos_t - real * sin_t], axis=0)
        )
    return exact_dot(halves(last_ref[...]), halves(jnp.concatenate(cols, axis=1)))


def product(left, right):
    return (left[0] * right[0] - left[1] * right[1], left[0] * right[1] + left[1] * right[0])


def conj_product(left, right):
    return (left[0] * right[0] + left[1] * right[1], left[0] * right[1] - left[1] * right[0])


def every(start, stride):
    return pl.ds(start, side, stride=stride)


def first_kernel(key_hbm, value_hbm, filt_hbm, query_hbm, cot_hbm, gain_hbm, *refs):
    sent_ref, query_t_ref, scaled_t_ref = refs[:3]
    key_ref, value_ref, filt_ref, query_ref, cot_ref, gain_ref, sems = refs[3:]
    sources = (filt_hbm, key_hbm, value_hbm, query_hbm, cot_hbm, gain_hbm)
    targets = (filt_ref, key_ref, value_ref, query_ref, cot_ref, gain_ref)
    copies = [
        pltpu.make_async_copy(a, b, sems.at[i]) for i, (a, b) in enumerate(zip(sources, targets))
    ]
    for copy in copies:
        copy.start()
    halves_of = [slice(h * side, (h + 1) * side) for h in range(2)]
    copies[0].wait()
    for h, cols in enumerate(halves_of):
        sent_ref[every(h, 4), :] = filt_ref[:, cols].T
    copies[1].wait()
    copies[2].wait()
    for h, cols in enumerate(halves_of):
        mixed = key_ref[:, cols].astype(jnp.float32) * value_ref[:, cols].astype(jnp.float32)
        sent_ref[every(2 + h, 4), :] = mixed.T
    for copy in copies[3:]:
        copy.wait()
    for h, cols in enumerate(halves_of):
        cot = cot_ref[:, cols].astype(jnp.float32)
        query_t_ref[cols, :] = query_ref[:, cols].T.astype(jnp.float32)
        scaled_t_ref[cols, :] = (cot * gain_ref[:, cols]).T


def conv_kernel(got_ref, first_ref, ahead_ref, back_ref, last_ref, twist_ref, out_ref, spec_ref):
    columns = [got_ref[every(u, 4), :] for u in range(4)]
    spectra = forward_spectra(columns, first_ref, ahead_ref, twist_ref)
    for u in range(4):
        spec_ref[u, 0] = spectra[u][0]
        spec_ref[u, 1] = spectra[u][1]
    both = [product(spectra[h], spectra[2 + h]) for h in range(2)]
    conv = inverse_columns(both, back_ref, last_ref, twist_ref)
    for h in range(2):
        out_ref[every(h, 2), :] = conv[:, h * side : (h + 1) * side]


def row_sums_kernel(conv_ref, query_t_ref, scaled_t_ref, out_ref):
    squares = jnp.zeros((1, side), jnp.float32)
    dots = jnp.zeros((1, side), jnp.float32)
    for h in range(2):
        cols = slice(h * side, (h + 1) * side)
        gated = conv_ref[every(h, 2), :] * query_t_ref[cols, :]
        squares = squares + jnp.sum(gated * gated, axis=0, keepdims=True)
        dots = dots + jnp.sum(scaled_t_ref[cols, :] * gated, axis=0, keepdims=True)
    out_ref[0:1, :] = squares
    out_ref[1:2, :] = dots


def row_scalars(sums_ref):
    squares = sums_ref[0, 0:1, :]
    dots = sums_ref[0, 1:2, :]
    for t in range(1, 4):
        squares = squares + sums_ref[t, 0:1, :]
        dots = dots + sums_ref[t, 1:2, :]
    inv_rms = lax.rsqrt(squares * (1.0 / channels) + norm_eps)
    return inv_rms, dots * (1.0 / channels)


def d_conv_kernel(conv_ref, query_t_ref, scaled_t_ref, sums_ref, out_ref):
    inv_rms, row_dot = row_scalars(sums_ref)
    pull = inv_rms * inv_rms * inv_rms * row_dot
    parts = []
    for h in range(2):
        cols = slice(h * side, (h + 1) * side)
        query = query_t_ref[cols, :]
        gated = conv_ref[every(h, 2), :] * query
        scaled = scaled_t_ref[cols, :]
        out_ref[every(h, 3), :] = (inv_rms * scaled - gated * pull) * query
        part = jnp.sum(scaled * gated * inv_rms, axis=1, keepdims=True)
        parts.append(jnp.broadcast_to(part, (side, side)).T)
    number = lax.broadcasted_iota(jnp.int32, (side, side), 0)
    out_ref[every(2, 3), :] = jnp.where((number & 2) == 0, parts[0], parts[1])


def row_outputs_kernel(
    conv_ref,
    query_t_ref,
    scaled_t_ref,
    sums_ref,
    gain_ref,
    got_ref,
    output_ref,
    grad_query_ref,
    gain_half_ref,
):
    inv_rms, row_dot = row_scalars(sums_ref)
    pull = inv_rms * inv_rms * inv_rms * row_dot
    for h in range(2):
        cols = slice(h * side, (h + 1) * side)
        conv = conv_ref[every(h, 2), :]
        gated = conv * query_t_ref[cols, :]
        scaled = scaled_t_ref[cols, :]
        normed = (gated * inv_rms).T
        output_ref[:, cols] = (normed * gain_ref[:, cols]).astype(jnp.bfloat16)
        grad = (inv_rms * scaled - gated * pull) * conv
        grad_query_ref[:, cols] = grad.T.astype(jnp.bfloat16)
    gain_half_ref[...] = jnp.sum(got_ref[every(2, 3), :], axis=0, keepdims=True)


def corr_kernel(
    got_ref, spec_ref, first_ref, ahead_ref, back_ref, last_ref, twist_ref, out_ref
):
    columns = [got_ref[every(h, 3), :] for h in range(2)]
    spectra = forward_spectra(columns, first_ref, ahead_ref, twist_ref)
    pairs = [
        conj_product((spec_ref[u, 0], spec_ref[u, 1]), spectra[u % 2]) for u in range(4)
    ]
    result = inverse_columns(pairs, back_ref, last_ref, twist_ref)
    for u in range(4):
        out_ref[every(u, 4), :] = result[:, u * side : (u + 1) * side]


def last_outputs_kernel(
    got_ref, key_ref, value_ref, grad_key_ref, grad_value_ref, grad_filter_ref
):
    for h in range(2):
        cols = slice(h * side, (h + 1) * side)
        d_mixed = got_ref[every(h, 4), :].T
        value = value_ref[:, cols].astype(jnp.float32)
        key = key_ref[:, cols].astype(jnp.float32)
        grad_key_ref[:, cols] = (d_mixed * value).astype(jnp.bfloat16)
        grad_value_ref[:, cols] = (d_mixed * key).astype(jnp.bfloat16)
        grad_filter_ref[:, cols] = got_ref[every(2 + h, 4), :].T


def call(kernel, outs, *operands, **options):
    moved = sum(math.prod(o.shape) * o.dtype.itemsize for o in operands)
    moved += sum(math.prod(o.shape) * o.dtype.itemsize for o in outs)
    result = pl.pallas_call(
        kernel,
        out_shape=outs,
        compiler_params=pltpu.CompilerParams(vmem_limit_bytes=vmem_bytes),
        cost_estimate=pl.CostEstimate(flops=0, bytes_accessed=moved, transcendentals=0),
        **options,
    )(*operands)
    return result


def f32(*shape):
    return jax.ShapeDtypeStruct(shape, jnp.float32)


def bf16(*shape):
    return jax.ShapeDtypeStruct(shape, jnp.bfloat16)


def swap(sent, rows):
    shape = (side, 1, rows * side) if rows == 3 else (side, rows, side)
    got = lax.all_to_all(
        sent.reshape(shape),
        "ctx",
        split_axis=0,
        concat_axis=0,
        axis_index_groups=[swap_order()],
        tiled=True,
    )
    return got.reshape(side * rows, side)


def per_device(gate_query, key_proj, value_proj, long_filter, out_gain, cotangent):
    *tables, twist = (jnp.asarray(t) for t in make_tables())
    wide = 2 * side
    gain = out_gain.reshape(1, wide)

    in_hbm = pl.BlockSpec(memory_space=pltpu.HBM)
    inputs = (key_proj, value_proj, long_filter, gate_query, cotangent, gain)
    sent, query_t, scaled_t = call(
        first_kernel,
        (f32(4 * side, side),) + (f32(wide, side),) * 2,
        *(pltpu.with_memory_space_constraint(x, pltpu.HBM) for x in inputs),
        in_specs=[in_hbm] * 6,
        scratch_shapes=[
            pltpu.VMEM((side, wide), jnp.bfloat16),
            pltpu.VMEM((side, wide), jnp.bfloat16),
            pltpu.VMEM((side, wide), jnp.float32),
            pltpu.VMEM((side, wide), jnp.bfloat16),
            pltpu.VMEM((side, wide), jnp.bfloat16),
            pltpu.VMEM((1, wide), jnp.float32),
            pltpu.SemaphoreType.DMA((6,)),
        ],
    )
    got = swap(sent, 4)
    sent, spectra = call(
        conv_kernel, (f32(wide, side), f32(4, 2, side, side)), got, *tables, twist
    )
    conv_t = swap(sent, 2)
    (sums,) = call(row_sums_kernel, (f32(2, side),), conv_t, query_t, scaled_t)
    sums = lax.all_gather(sums, "tp")
    (sent,) = call(d_conv_kernel, (f32(3 * side, side),), conv_t, query_t, scaled_t, sums)
    got = swap(sent, 3)
    output, grad_query, gain_half = call(
        row_outputs_kernel,
        (bf16(side, wide), bf16(side, wide), f32(1, side)),
        conv_t,
        query_t,
        scaled_t,
        sums,
        gain,
        got,
    )
    other_half = lax.ppermute(gain_half, "ctx", [(i, i ^ 1) for i in range(side)])
    odd = (lax.axis_index("ctx") & 1) == 1
    grad_gain = jnp.concatenate(
        [jnp.where(odd, other_half, gain_half), jnp.where(odd, gain_half, other_half)], axis=1
    )
    (sent,) = call(
        corr_kernel,
        (f32(4 * side, side),),
        got,
        spectra,
        *tables,
        twist,
    )
    got = swap(sent, 4)
    grad_key, grad_value, grad_filter = call(
        last_outputs_kernel,
        (bf16(side, wide), bf16(side, wide), f32(side, wide)),
        got,
        key_proj,
        value_proj,
    )
    grad_gain = (grad_gain / gain).reshape(wide)
    return (output, grad_query, grad_key, grad_value, grad_filter, grad_gain)


def solution(mesh):
    both = P("ctx", "tp")
    return jax.shard_map(
        per_device,
        mesh=mesh,
        in_specs=(both, both, both, both, P("tp"), both),
        out_specs=(both, both, both, both, both, P("tp")),
        check_vma=False,
    )
```

```python
import math

import jax
import jax.numpy as jnp
import numpy as np
from jax import lax
from jax.experimental import pallas as pl
from jax.experimental.pallas import tpu as pltpu
from jax.sharding import PartitionSpec as P

norm_eps = 1e-06
side = 128
length = side * side
channels = 1024
ctx_sizes = (2, 16, 4)
vmem_bytes = 40 * 1024 * 1024


def swap_order():
    grid = np.arange(side).reshape(ctx_sizes).transpose(1, 2, 0)
    grid = np.roll(grid, (7, 2, 1), axis=(0, 1, 2))
    return grid[[0] + list(range(15, 0, -1))].reshape(-1).tolist()


def make_tables():
    block = np.array(swap_order())
    idx = np.arange(side)
    ang_a = 2.0 * math.pi * ((idx[:, None] + 0.25) * block[None, :] / side)
    cos_a, sin_a = np.cos(ang_a), np.sin(ang_a)
    first = np.concatenate([cos_a, sin_a], axis=0)
    scale = 1.0 / length / math.sqrt(length)
    last = np.concatenate([cos_a.T, sin_a.T], axis=1) * scale
    ang_t = 2.0 * math.pi * ((idx[:, None] + 0.25) * idx[None, :] / length)
    twist = np.stack([np.cos(ang_t), np.sin(ang_t)]).astype(np.float32)
    ang_b = 2.0 * math.pi * (idx[:, None] * idx[None, :] % side) / side
    cos_b, sin_b = np.cos(ang_b), np.sin(ang_b)
    ahead = np.block([[cos_b, sin_b], [-sin_b, cos_b]])
    back = np.block([[cos_b, -sin_b], [sin_b, cos_b]])
    return tuple(t.astype(np.float32) for t in (first, ahead, back, last)) + (twist,)


def halves(value):
    high = value.astype(jnp.bfloat16)
    low = (value - high.astype(jnp.float32)).astype(jnp.bfloat16)
    return high, low


def dot(left, right):
    return jnp.dot(left, right, preferred_element_type=jnp.float32)


def exact_dot(left, right):
    (left_high, left_low), (right_high, right_low) = left, right
    return dot(left_high, right_high) + (dot(left_high, right_low) + dot(left_low, right_high))


def forward_spectra(columns, first_ref, ahead_ref, twist_ref):
    count = len(columns)
    high, low = halves(jnp.concatenate(columns, axis=1))
    first_high, first_low = halves(first_ref[...])
    mid = dot(jnp.concatenate([first_high, first_high], axis=1), jnp.concatenate([high, low], axis=0))
    mid = mid + dot(first_low, high)
    cos_t, sin_t = twist_ref[0], twist_ref[1]
    rows = []
    for u in range(count):
        real = mid[:side, u * side : (u + 1) * side]
        imag = mid[side:, u * side : (u + 1) * side]
        rows.append(
            jnp.concatenate([real * cos_t - imag * sin_t, real * sin_t + imag * cos_t], axis=1)
        )
    out = exact_dot(halves(jnp.concatenate(rows, axis=0)), halves(ahead_ref[...]))
    return [
        (out[u * side : (u + 1) * side, :side], out[u * side : (u + 1) * side, side:])
        for u in range(count)
    ]


def inverse_columns(spectra, back_ref, last_ref, twist_ref):
    count = len(spectra)
    stacked = jnp.concatenate([jnp.concatenate(pair, axis=1) for pair in spectra], axis=0)
    mid = exact_dot(halves(stacked), halves(back_ref[...]))
    cos_t, sin_t = twist_ref[0], twist_ref[1]
    cols = []
    for u in range(count):
        real = mid[u * side : (u + 1) * side, :side]
        imag = mid[u * side : (u + 1) * side, side:]
        cols.append(
            jnp.concatenate([real * cos_t + imag * sin_t, imag * cos_t - real * sin_t], axis=0)
        )
    return exact_dot(halves(last_ref[...]), halves(jnp.concatenate(cols, axis=1)))


def product(left, right):
    return (left[0] * right[0] - left[1] * right[1], left[0] * right[1] + left[1] * right[0])


def conj_product(left, right):
    return (left[0] * right[0] + left[1] * right[1], left[0] * right[1] - left[1] * right[0])


def every(start, stride):
    return pl.ds(start, side, stride=stride)


def first_kernel(key_hbm, value_hbm, filt_hbm, query_hbm, cot_hbm, gain_hbm, *refs):
    sent_ref, query_t_ref, scaled_t_ref = refs[:3]
    key_ref, value_ref, filt_ref, query_ref, cot_ref, gain_ref, sems = refs[3:]
    sources = (filt_hbm, key_hbm, value_hbm, query_hbm, cot_hbm, gain_hbm)
    targets = (filt_ref, key_ref, value_ref, query_ref, cot_ref, gain_ref)
    copies = [
        pltpu.make_async_copy(a, b, sems.at[i]) for i, (a, b) in enumerate(zip(sources, targets))
    ]
    for copy in copies:
        copy.start()
    halves_of = [slice(h * side, (h + 1) * side) for h in range(2)]
    copies[0].wait()
    for h, cols in enumerate(halves_of):
        sent_ref[every(h, 4), :] = filt_ref[:, cols].T
    copies[1].wait()
    copies[2].wait()
    for h, cols in enumerate(halves_of):
        mixed = key_ref[:, cols].astype(jnp.float32) * value_ref[:, cols].astype(jnp.float32)
        sent_ref[every(2 + h, 4), :] = mixed.T
    for copy in copies[3:]:
        copy.wait()
    for h, cols in enumerate(halves_of):
        cot = cot_ref[:, cols].astype(jnp.float32)
        query_t_ref[cols, :] = query_ref[:, cols].T.astype(jnp.float32)
        scaled_t_ref[cols, :] = (cot * gain_ref[:, cols]).T


def conv_kernel(got_ref, first_ref, ahead_ref, back_ref, last_ref, twist_ref, out_ref, spec_ref):
    columns = [got_ref[every(u, 4), :] for u in range(4)]
    spectra = forward_spectra(columns, first_ref, ahead_ref, twist_ref)
    for u in range(4):
        spec_ref[u, 0] = spectra[u][0]
        spec_ref[u, 1] = spectra[u][1]
    both = [product(spectra[h], spectra[2 + h]) for h in range(2)]
    conv = inverse_columns(both, back_ref, last_ref, twist_ref)
    for h in range(2):
        out_ref[every(h, 2), :] = conv[:, h * side : (h + 1) * side]


def row_sums_kernel(conv_ref, query_t_ref, scaled_t_ref, out_ref):
    squares = jnp.zeros((1, side), jnp.float32)
    dots = jnp.zeros((1, side), jnp.float32)
    for h in range(2):
        cols = slice(h * side, (h + 1) * side)
        gated = conv_ref[every(h, 2), :] * query_t_ref[cols, :]
        squares = squares + jnp.sum(gated * gated, axis=0, keepdims=True)
        dots = dots + jnp.sum(scaled_t_ref[cols, :] * gated, axis=0, keepdims=True)
    out_ref[0:1, :] = squares
    out_ref[1:2, :] = dots


def row_scalars(sums_ref):
    squares = sums_ref[0, 0:1, :]
    dots = sums_ref[0, 1:2, :]
    for t in range(1, 4):
        squares = squares + sums_ref[t, 0:1, :]
        dots = dots + sums_ref[t, 1:2, :]
    inv_rms = lax.rsqrt(squares * (1.0 / channels) + norm_eps)
    return inv_rms, dots * (1.0 / channels)


def d_conv_kernel(conv_ref, query_t_ref, scaled_t_ref, sums_ref, out_ref):
    inv_rms, row_dot = row_scalars(sums_ref)
    pull = inv_rms * inv_rms * inv_rms * row_dot
    parts = []
    for h in range(2):
        cols = slice(h * side, (h + 1) * side)
        query = query_t_ref[cols, :]
        gated = conv_ref[every(h, 2), :] * query
        scaled = scaled_t_ref[cols, :]
        out_ref[every(h, 3), :] = (inv_rms * scaled - gated * pull) * query
        part = jnp.sum(scaled * gated * inv_rms, axis=1, keepdims=True)
        parts.append(jnp.broadcast_to(part, (side, side)).T)
    number = lax.broadcasted_iota(jnp.int32, (side, side), 0)
    out_ref[every(2, 3), :] = jnp.where((number & 2) == 0, parts[0], parts[1])


def row_outputs_kernel(
    conv_ref,
    query_t_ref,
    scaled_t_ref,
    sums_ref,
    gain_ref,
    got_ref,
    output_ref,
    grad_query_ref,
    gain_half_ref,
):
    inv_rms, row_dot = row_scalars(sums_ref)
    pull = inv_rms * inv_rms * inv_rms * row_dot
    for h in range(2):
        cols = slice(h * side, (h + 1) * side)
        conv = conv_ref[every(h, 2), :]
        gated = conv * query_t_ref[cols, :]
        scaled = scaled_t_ref[cols, :]
        normed = (gated * inv_rms).T
        output_ref[:, cols] = (normed * gain_ref[:, cols]).astype(jnp.bfloat16)
        grad = (inv_rms * scaled - gated * pull) * conv
        grad_query_ref[:, cols] = grad.T.astype(jnp.bfloat16)
    gain_half_ref[...] = jnp.sum(got_ref[every(2, 3), :], axis=0, keepdims=True)


def corr_kernel(
    got_ref, spec_ref, first_ref, ahead_ref, back_ref, last_ref, twist_ref, out_ref
):
    columns = [got_ref[every(h, 3), :] for h in range(2)]
    spectra = forward_spectra(columns, first_ref, ahead_ref, twist_ref)
    pairs = [
        conj_product((spec_ref[u, 0], spec_ref[u, 1]), spectra[u % 2]) for u in range(4)
    ]
    result = inverse_columns(pairs, back_ref, last_ref, twist_ref)
    for u in range(4):
        out_ref[every(u, 4), :] = result[:, u * side : (u + 1) * side]


def last_outputs_kernel(
    got_ref, key_ref, value_ref, grad_key_ref, grad_value_ref, grad_filter_ref
):
    for h in range(2):
        cols = slice(h * side, (h + 1) * side)
        d_mixed = got_ref[every(h, 4), :].T
        value = value_ref[:, cols].astype(jnp.float32)
        key = key_ref[:, cols].astype(jnp.float32)
        grad_key_ref[:, cols] = (d_mixed * value).astype(jnp.bfloat16)
        grad_value_ref[:, cols] = (d_mixed * key).astype(jnp.bfloat16)
        grad_filter_ref[:, cols] = got_ref[every(2 + h, 4), :].T


def call(kernel, outs, *operands, **options):
    moved = sum(math.prod(o.shape) * o.dtype.itemsize for o in operands)
    moved += sum(math.prod(o.shape) * o.dtype.itemsize for o in outs)
    result = pl.pallas_call(
        kernel,
        out_shape=outs,
        compiler_params=pltpu.CompilerParams(vmem_limit_bytes=vmem_bytes),
        cost_estimate=pl.CostEstimate(flops=0, bytes_accessed=moved, transcendentals=0),
        **options,
    )(*operands)
    return result


def f32(*shape):
    return jax.ShapeDtypeStruct(shape, jnp.float32)


def bf16(*shape):
    return jax.ShapeDtypeStruct(shape, jnp.bfloat16)


def swap(sent, rows):
    shape = (side, 1, rows * side) if rows == 3 else (side, rows, side)
    got = lax.all_to_all(
        sent.reshape(shape),
        "ctx",
        split_axis=0,
        concat_axis=0,
        axis_index_groups=[swap_order()],
        tiled=True,
    )
    return got.reshape(side * rows, side)


def per_device(gate_query, key_proj, value_proj, long_filter, out_gain, cotangent):
    *tables, twist = (jnp.asarray(t) for t in make_tables())
    wide = 2 * side
    gain = out_gain.reshape(1, wide)

    in_hbm = pl.BlockSpec(memory_space=pltpu.HBM)
    inputs = (key_proj, value_proj, long_filter, gate_query, cotangent, gain)
    sent, query_t, scaled_t = call(
        first_kernel,
        (f32(4 * side, side),) + (f32(wide, side),) * 2,
        *(pltpu.with_memory_space_constraint(x, pltpu.HBM) for x in inputs),
        in_specs=[in_hbm] * 6,
        scratch_shapes=[
            pltpu.VMEM((side, wide), jnp.bfloat16),
            pltpu.VMEM((side, wide), jnp.bfloat16),
            pltpu.VMEM((side, wide), jnp.float32),
            pltpu.VMEM((side, wide), jnp.bfloat16),
            pltpu.VMEM((side, wide), jnp.bfloat16),
            pltpu.VMEM((1, wide), jnp.float32),
            pltpu.SemaphoreType.DMA((6,)),
        ],
    )
    got = swap(sent, 4)
    sent, spectra = call(
        conv_kernel, (f32(wide, side), f32(4, 2, side, side)), got, *tables, twist
    )
    conv_t = swap(sent, 2)
    (sums,) = call(row_sums_kernel, (f32(2, side),), conv_t, query_t, scaled_t)
    sums = lax.all_gather(sums, "tp")
    (sent,) = call(d_conv_kernel, (f32(3 * side, side),), conv_t, query_t, scaled_t, sums)
    got = swap(sent, 3)
    output, grad_query, gain_half = call(
        row_outputs_kernel,
        (bf16(side, wide), bf16(side, wide), f32(1, side)),
        conv_t,
        query_t,
        scaled_t,
        sums,
        gain,
        got,
    )
    other_half = lax.ppermute(gain_half, "ctx", [(i, i ^ 1) for i in range(side)])
    odd = (lax.axis_index("ctx") & 1) == 1
    grad_gain = jnp.concatenate(
        [jnp.where(odd, other_half, gain_half), jnp.where(odd, gain_half, other_half)], axis=1
    )
    (sent,) = call(
        corr_kernel,
        (f32(4 * side, side),),
        got,
        spectra,
        *tables,
        twist,
    )
    got = swap(sent, 4)
    grad_key, grad_value, grad_filter = call(
        last_outputs_kernel,
        (bf16(side, wide), bf16(side, wide), f32(side, wide)),
        got,
        key_proj,
        value_proj,
    )
    grad_gain = (grad_gain / gain).reshape(wide)
    return (output, grad_query, grad_key, grad_value, grad_filter, grad_gain)


def solution(mesh):
    both = P("ctx", "tp")
    return jax.shard_map(
        per_device,
        mesh=mesh,
        in_specs=(both, both, both, both, P("tp"), both),
        out_specs=(both, both, both, both, both, P("tp")),
        check_vma=False,
    )
```
